256 devices in a mesh: dp: 2 (over core), context: 128 (over x, z, y).
Axes of the slice: x: 4, y: 4, z: 8, core: 2. Of those that a mesh axis runs over, the one named last changes fastest.
Arguments:
- query_input: float32 [2, 2048, 16384], P('dp', None, 'context'), may hold values from -6 to 6
- key_input: float32 [2, 2048, 16384], P('dp', None, 'context'), may hold values from -6 to 6
- value_input: float32 [2, 2048, 16384], P('dp', None, 'context'), may hold values from -6 to 6
- filters: float32 [2048, 16384], P('context'), may hold values from -2 to 2, as said below
- cotangent: float32 [2, 2048, 16384], P('dp', None, 'context'), may hold values from -6 to 6
Outputs:
- gated_output: float32 [2, 2048, 16384], P('dp', None, 'context')
- grad_query: float32 [2, 2048, 16384], P('dp', None, 'context')
- grad_key: float32 [2, 2048, 16384], P('dp', None, 'context')
- grad_value: float32 [2, 2048, 16384], P('dp', None, 'context')
- grad_filter: float32 [2048, 16384], P('context')
The draws below stay inside these ranges and needn't reach their ends.
Inputs may be any that keep to these rules, and one draw needn't show every extreme that they name: `filters`: real-valued filter taps, one for each channel and lag.
All inputs are finite; a program needn't handle non-finite values.
Results may differ from the reference program's by a relative error of at most 0.000098.
Values sent between devices are 32-bit elements; how exact they have to be, the bound alone decides.
A program may use at most 128 MiB of HBM per device.

```python
import math
import jax
import jax.numpy as jnp
from jax import lax

C = 2048
SEQS = 2
LENGTH = 16384


def draw_filters(key, part):
    key = jax.random.fold_in(key, 7)
    key_fast, key_span, key_rate, key_noise = jax.random.split(key, 4)
    positions = jnp.arange(LENGTH, dtype=jnp.float32)[None, :]
    fast = jax.random.bernoulli(key_fast, 0.5, (C, 1))
    noise = jnp.clip(jax.random.normal(key_noise, (C, LENGTH)), -6.0, 6.0)
    span = jax.random.uniform(key_span, (C, 1), minval=30.0, maxval=50.0)
    rate = jax.random.uniform(key_rate, (C, 1), minval=0.2, maxval=2.0)
    fast_env = jnp.exp(-positions / span) * jnp.sqrt(2.0 / span)
    slow_env = jnp.exp(-rate * positions / LENGTH) * jnp.sqrt(2.0 * rate / LENGTH)
    envelope = jnp.where(fast, fast_env + 0.05 * slow_env, slow_env)
    return (noise * envelope).astype(jnp.float32)


def levels(rng, shape, pieces, low, largest):
    gain, own = 1.0, jax.random.fold_in(rng, 6)
    for position, shards_of in pieces:
        steps = jnp.exp(jax.random.uniform(jax.random.fold_in(own, position), (shards_of,), jnp.float32, low / len(pieces), largest / len(pieces)))
        gain = gain * jnp.repeat(steps, shape[position] // shards_of).reshape([-1 if axis == position else 1 for axis in range(len(shape))])
    return gain


def gaussian(own_key, extent, deviation, bound, pieces=(), kind=jnp.bfloat16):
    drawn = deviation * jax.random.normal(own_key, extent, jnp.float32)
    if pieces:
        drawn = drawn * levels(own_key, extent, pieces, -0.22, 0.18)
    return jnp.clip(drawn, -bound, bound).astype(kind)


def setup_inputs(seed: int = 0) -> dict:
    key_of = jax.random.split(jax.random.key(seed), 6)
    query_input = gaussian(key_of[0], (SEQS, C, LENGTH), 1.0, 6.0, ((0, 2), (2, 128)), jnp.float32)
    key_input = gaussian(key_of[1], (SEQS, C, LENGTH), 1.0, 6.0, ((0, 2), (2, 128)), jnp.float32)
    value_input = gaussian(key_of[2], (SEQS, C, LENGTH), 1.0, 6.0, ((0, 2), (2, 128)), jnp.float32)
    filters = draw_filters(jax.random.fold_in(key_of[5], 71), 0)
    cotangent = gaussian(key_of[4], (SEQS, C, LENGTH), 1.0, 6.0, ((0, 2), (2, 128)), jnp.float32)
    return {"query_input": query_input, "key_input": key_input, "value_input": value_input, "filters": filters, "cotangent": cotangent}


def block_pass(operands):
    query_block, key_block, value_block, filter_block, grad_block = operands
    total_size = 2 * LENGTH
    product = key_block * value_block
    conv_grad = grad_block * query_block
    spec_product = jnp.fft.rfft(product, n=total_size, axis=-1)
    spec_filter = jnp.fft.rfft(filter_block, n=total_size, axis=-1)[None]
    spec_grad = jnp.fft.rfft(conv_grad, n=total_size, axis=-1)
    conv = jnp.fft.irfft(spec_filter * spec_product, n=total_size, axis=-1)[..., :LENGTH]
    product_grad = jnp.fft.irfft(jnp.conj(spec_filter) * spec_grad, n=total_size, axis=-1)[..., :LENGTH]
    filter_grad = jnp.fft.irfft(jnp.conj(spec_product) * spec_grad, n=total_size, axis=-1)[..., :LENGTH]
    filter_grad = lax.optimization_barrier(jnp.sum(filter_grad, axis=0)) * (1.0 / math.sqrt(SEQS * LENGTH))
    return (query_block * conv, grad_block * conv, product_grad * value_block, product_grad * key_block, filter_grad)

def reference(query_input, key_input, value_input, filters, cotangent):
    block = min(C, 128)
    blocks = C // block

    def split(array):
        return array.reshape(SEQS, blocks, block, LENGTH).transpose(1, 0, 2, 3)

    def join(array):
        return array.transpose(1, 0, 2, 3).reshape(SEQS, C, LENGTH)
    results = lax.map(block_pass, (split(query_input), split(key_input), split(value_input), filters.reshape(blocks, block, LENGTH), split(cotangent)))
    gated, grad_q, grad_k, grad_v, grad_f = results
    return (join(gated), join(grad_q), join(grad_k), join(grad_v), grad_f.reshape(C, LENGTH))
```

```python
import functools
import math

import jax
import jax.numpy as jnp
import ml_dtypes
import numpy as np
from jax import lax
from jax.experimental import pallas as pl
from jax.experimental.pallas import tpu as pltpu
from jax.sharding import PartitionSpec as P

MESH = pl.DeviceIdType.MESH
F32 = jnp.float32
BF16 = jnp.bfloat16
N = 128
SUB = 8
CHUNKS = 2
ROWS = 2 * SUB
LANES = 128


def halves(table):
    high = table.astype(ml_dtypes.bfloat16)
    low = (table - high.astype(np.float64)).astype(ml_dtypes.bfloat16)
    return high, low


def tables():
    steps = np.arange(N, dtype=np.float64)
    total = N * N
    outer = 2.0 * math.pi / N * (steps[:, None] + 0.25) * steps[None, :]
    twist = 2.0 * math.pi / total * (steps[:, None] + 0.25) * steps[None, :]
    inner = 2.0 * math.pi / N * ((steps[:, None] * steps[None, :]) % N)
    high, low = halves(np.concatenate([np.cos(outer), -np.sin(outer)], axis=0))
    first = np.concatenate([high, low, high], axis=1)
    high, low = halves(np.concatenate([np.cos(outer.T), -np.sin(outer.T)], axis=1) / total)
    last = np.concatenate([high, low, high], axis=1)
    cos, sin = np.cos(inner), np.sin(inner)
    ahead = np.block([[cos, -sin], [sin, cos]])
    back = np.block([[cos, sin], [-sin, cos]])
    middle = np.stack([*halves(ahead), *halves(back)])
    turn = np.stack([np.cos(twist), np.sin(twist)]).astype(np.float32)
    return first, last, middle, turn


def split(value):
    high = value.astype(BF16)
    low = (value - high.astype(F32)).astype(BF16)
    return high, low


def dot(left, right):
    return jnp.dot(left, right, preferred_element_type=F32)


def columns(value, index):
    return value[:, index * LANES : (index + 1) * LANES]


def by_inner(pairs, high, low):
    stacked = jnp.concatenate([jnp.concatenate(pair, axis=1) for pair in pairs], axis=0)
    stacked_high, stacked_low = split(stacked)
    result = dot(stacked_high, high) + dot(stacked_low, high) + dot(stacked_high, low)
    return [
        (result[i * N : (i + 1) * N, :N], result[i * N : (i + 1) * N, N:])
        for i in range(len(pairs))
    ]


def forward(signals, first, high, low, cos, sin):
    signal_high, signal_low = split(jnp.concatenate(signals, axis=1))
    mixed = dot(first, jnp.concatenate([signal_high, signal_high, signal_low], axis=0))
    pairs = []
    for i in range(len(signals)):
        re, im = columns(mixed[:N], i), columns(mixed[N:], i)
        pairs.append((re * cos + im * sin, im * cos - re * sin))
    return by_inner(pairs, high, low)


def inverse(spectra, last, high, low, cos, sin):
    turned_re, turned_im = [], []
    for re, im in by_inner(spectra, high, low):
        turned_re.append(re * cos - im * sin)
        turned_im.append(re * sin + im * cos)
    stacked = jnp.concatenate(
        [jnp.concatenate(turned_re, axis=1), jnp.concatenate(turned_im, axis=1)], axis=0
    )
    stacked_high, stacked_low = split(stacked)
    return dot(last, jnp.concatenate([stacked_high, stacked_high, stacked_low], axis=0))


def times(a, b):
    return (a[0] * b[0] - a[1] * b[1], a[0] * b[1] + a[1] * b[0])


def conj_times(a, b):
    return (a[0] * b[0] + a[1] * b[1], a[0] * b[1] - a[1] * b[0])


def exchange_kernel(
    size,
    q_hbm, k_hbm, v_hbm, c_hbm, filt_hbm, first_hbm, last_hbm, middle_hbm, turn_hbm,
    back_ref, own_ref, other_ref,
    q_ref, k_ref, v_ref, c_ref, filt_ref, first_ref, last_ref, middle_ref, turn_ref,
    send_ref, recv_ref, out_ref, spec_ref,
    load_sems, in_send, in_recv, out_send, out_recv, pair_send, pair_recv,
):
    me = lax.axis_index("context")
    pair = lax.axis_index("dp")

    def loader(i, source, target):
        return pltpu.make_async_copy(source, target, load_sems.at[i])

    loads = [
        loader(i, source, target)
        for i, (source, target) in enumerate(
            [
                (k_hbm, k_ref), (v_hbm, v_ref), (c_hbm, c_ref), (q_hbm, q_ref),
                (filt_hbm, filt_ref), (first_hbm, first_ref), (last_hbm, last_ref),
                (middle_hbm, middle_ref), (turn_hbm, turn_ref),
            ]
        )
    ]
    for load in loads:
        load.start()

    barrier = pltpu.get_barrier_semaphore()

    @pl.loop(1, size)
    def _(step):
        pl.semaphore_signal(
            barrier, inc=1, device_id=(pair, lax.rem(me + step, size)), device_id_type=MESH
        )

    pl.semaphore_signal(barrier, inc=1, device_id=(1 - pair, me), device_id_type=MESH)

    for load in loads[:4]:
        load.wait()

    def rows_of(peer):
        return pl.ds(pl.multiple_of(peer * ROWS, ROWS), ROWS)

    def products(chunk):
        @pl.loop(0, size, unroll=8)
        def _(peer):
            base = pl.multiple_of(peer * ROWS, ROWS)
            send_ref[chunk, pl.ds(base, SUB), :] = k_ref[peer, chunk] * v_ref[peer, chunk]
            send_ref[chunk, pl.ds(base + SUB, SUB), :] = c_ref[peer, chunk] * q_ref[peer, chunk]

    def send_all(chunk, source, target, send_sem, recv_sem):
        target[chunk, rows_of(me), :] = source[chunk, rows_of(me), :]

        @pl.loop(1, size)
        def _(step):
            peer = lax.rem(me + step, size)
            pltpu.make_async_remote_copy(
                src_ref=source.at[chunk, rows_of(peer), :],
                dst_ref=target.at[chunk, rows_of(me), :],
                send_sem=send_sem.at[chunk],
                recv_sem=recv_sem.at[chunk],
                device_id=(pair, peer),
                device_id_type=MESH,
            ).start()

    def await_all(chunk, ref, sem):
        part = ref.at[chunk, pl.ds(0, (size - 1) * ROWS), :]
        pltpu.make_async_copy(part, part, sem.at[chunk]).wait()

    products(0)
    pl.semaphore_wait(barrier, size)
    send_all(0, send_ref, recv_ref, in_send, in_recv)
    products(1)
    send_all(1, send_ref, recv_ref, in_send, in_recv)

    for load in loads[4:]:
        load.wait()

    def ahead(signals):
        return forward(
            signals, first_ref[...], middle_ref[0], middle_ref[1], turn_ref[0], turn_ref[1]
        )

    for chunk in range(CHUNKS):
        @pl.loop(0, SUB // 4)
        def _(step):
            at = step * 4
            signals = [filt_ref[chunk, pl.ds(at + i, N, stride=SUB), :] for i in range(4)]
            for i, (re, im) in enumerate(ahead(signals)):
                spec_ref[chunk, at + i, 0] = re
                spec_ref[chunk, at + i, 1] = im

    def convolve(chunk):
        @pl.loop(0, SUB // 2)
        def _(step):
            at = step * 2
            signals = [
                recv_ref[chunk, pl.ds(at + i + SUB * signal, N, stride=ROWS), :]
                for i in range(2)
                for signal in range(2)
            ]
            spectra = ahead(signals)
            mixed = []
            for i in range(2):
                product, grad = spectra[2 * i], spectra[2 * i + 1]
                filt = (spec_ref[chunk, at + i, 0], spec_ref[chunk, at + i, 1])
                mixed.append(times(filt, product))
                mixed.append(conj_times(filt, grad))
                mixed.append(conj_times(product, grad))
            results = inverse(
                mixed, last_ref[...], middle_ref[2], middle_ref[3], turn_ref[0], turn_ref[1]
            )
            for i in range(2):
                out_ref[chunk, pl.ds(at + i, N, stride=ROWS), :] = columns(results, 3 * i)
                out_ref[chunk, pl.ds(at + i + SUB, N, stride=ROWS), :] = columns(
                    results, 3 * i + 1
                )
                own_ref[chunk, pl.ds(at + i, N, stride=SUB), :] = columns(results, 3 * i + 2)

    def pair_copy(chunk):
        return pltpu.make_async_remote_copy(
            src_ref=own_ref.at[chunk],
            dst_ref=other_ref.at[chunk],
            send_sem=pair_send.at[chunk],
            recv_sem=pair_recv.at[chunk],
            device_id=(1 - pair, me),
            device_id_type=MESH,
        )

    for chunk in range(CHUNKS):
        await_all(chunk, recv_ref, in_recv)
        convolve(chunk)
        send_all(chunk, out_ref, back_ref, out_send, out_recv)
        pair_copy(chunk).start()

    for chunk in range(CHUNKS):
        pair_copy(chunk).wait()
        await_all(chunk, send_ref, in_send)
        await_all(chunk, out_ref, out_send)
    for chunk in range(CHUNKS):
        await_all(chunk, back_ref, out_recv)


def gate_kernel(
    scale, q_ref, k_ref, v_ref, c_ref, back_ref, own_ref, other_ref,
    gated_ref, grad_q_ref, grad_k_ref, grad_v_ref, grad_f_ref,
):
    conv, back = back_ref[0, :, 0], back_ref[0, :, 1]
    gated_ref[:, 0] = q_ref[:, 0] * conv
    grad_q_ref[:, 0] = c_ref[:, 0] * conv
    grad_k_ref[:, 0] = v_ref[:, 0] * back
    grad_v_ref[:, 0] = k_ref[:, 0] * back
    grad_f_ref[...] = (own_ref[...] + other_ref[...]) * scale


def on_device(query_input, key_input, value_input, filters, cotangent):
    size = lax.axis_size("context")
    channels = query_input.shape[1]
    rows, length = filters.shape
    scale = 1.0 / math.sqrt(lax.axis_size("dp") * length)
    token_shape = (size, CHUNKS, SUB, LANES)
    tokens = [
        array.reshape(token_shape) for array in (query_input, key_input, value_input, cotangent)
    ]
    taps = filters.reshape(CHUNKS, SUB, size, LANES).transpose(0, 2, 1, 3)
    taps = taps.reshape(CHUNKS, size * SUB, LANES)
    constants = [jnp.asarray(table) for table in tables()]

    any_spec = pl.BlockSpec(memory_space=pl.ANY)
    vmem_spec = pl.BlockSpec(memory_space=pltpu.VMEM)
    wide = (CHUNKS, size * ROWS, LANES)
    narrow = (CHUNKS, size * SUB, LANES)
    per_chunk = pltpu.SemaphoreType.DMA((CHUNKS,))
    back, own, other = pl.pallas_call(
        functools.partial(exchange_kernel, size),
        out_shape=[
            jax.ShapeDtypeStruct(wide, F32),
            jax.ShapeDtypeStruct(narrow, F32),
            jax.ShapeDtypeStruct(narrow, F32),
        ],
        in_specs=[any_spec] * 9,
        out_specs=[vmem_spec] * 3,
        scratch_shapes=[pltpu.VMEM(token_shape, F32) for _ in range(4)]
        + [pltpu.VMEM(narrow, F32)]
        + [pltpu.VMEM(table.shape, table.dtype) for table in constants]
        + [
            pltpu.VMEM(wide, F32),
            pltpu.VMEM(wide, F32),
            pltpu.VMEM(wide, F32),
            pltpu.VMEM((CHUNKS, SUB, 2, N, LANES), F32),
            pltpu.SemaphoreType.DMA((9,)),
        ]
        + [per_chunk] * 6,
        compiler_params=pltpu.CompilerParams(
            collective_id=0, has_side_effects=True, vmem_limit_bytes=40 * 2**20
        ),
        name="exchange",
    )(*tokens, taps, *constants)

    block = 32
    def token_block(i, chunk):
        return (i, chunk, 0, 0)
    token_spec = pl.BlockSpec((block, 1, SUB, LANES), token_block)
    filter_spec = pl.BlockSpec((1, block * SUB, LANES), lambda i, chunk: (chunk, i, 0))
    back_spec = pl.BlockSpec(
        (1, block, 2, SUB, LANES), lambda i, chunk: (chunk, i, 0, 0, 0)
    )
    results = pl.pallas_call(
        functools.partial(gate_kernel, scale),
        grid=(size // block, CHUNKS),
        out_shape=[jax.ShapeDtypeStruct(token_shape, F32)] * 4
        + [jax.ShapeDtypeStruct(narrow, F32)],
        in_specs=[token_spec] * 4 + [back_spec, filter_spec, filter_spec],
        out_specs=[token_spec] * 4 + [filter_spec],
        name="gate",
    )(*tokens, back.reshape(CHUNKS, size, 2, SUB, LANES), own, other)
    per_token = [array.reshape(1, channels, LANES) for array in results[:4]]
    grad_filter = results[4].reshape(CHUNKS, size, SUB, LANES).transpose(0, 2, 1, 3)
    return (*per_token, grad_filter.reshape(rows, length))


def solution(mesh):
    token = P("dp", None, "context")
    taps = P("context", None)
    return jax.shard_map(
        on_device,
        mesh=mesh,
        in_specs=(token, token, token, taps, token),
        out_specs=(token, token, token, token, taps),
        check_vma=False,
    )
```

```python
import functools
import math

import jax
import jax.numpy as jnp
import numpy as np
from jax import lax
from jax.experimental import pallas as pl
from jax.experimental.pallas import tpu as pltpu
from jax.sharding import PartitionSpec as P

MESH = pl.DeviceIdType.MESH
F32 = jnp.float32
BF16 = jnp.bfloat16
N = 128
SUB = 8
CHUNKS = 2
ROWS = 2 * SUB
LANES = 128


def tables():
    steps = np.arange(N, dtype=np.float64)
    total = N * N
    outer = 2.0 * math.pi / N * (steps[:, None] + 0.25) * steps[None, :]
    twist = 2.0 * math.pi / total * (steps[:, None] + 0.25) * steps[None, :]
    inner = 2.0 * math.pi / N * ((steps[:, None] * steps[None, :]) % N)
    first = np.concatenate([np.cos(outer), -np.sin(outer)], axis=0)
    last = np.concatenate([np.cos(outer.T), -np.sin(outer.T)], axis=1) / total
    cos, sin = np.cos(inner), np.sin(inner)
    middle = np.stack([np.block([[cos, -sin], [sin, cos]]), np.block([[cos, sin], [-sin, cos]])])
    turn = np.stack([np.cos(twist), np.sin(twist)])
    return [table.astype(np.float32) for table in (first, last, middle, turn)]


def split(value):
    high = value.astype(BF16)
    low = (value - high.astype(F32)).astype(BF16)
    return high, low


def dot(left, right):
    return jnp.dot(left, right, preferred_element_type=F32)


def columns(value, index):
    return value[:, index * LANES : (index + 1) * LANES]


def by_inner(pairs, high, low):
    stacked = jnp.concatenate([jnp.concatenate(pair, axis=1) for pair in pairs], axis=0)
    stacked_high, stacked_low = split(stacked)
    result = dot(stacked_high, high) + dot(stacked_low, high) + dot(stacked_high, low)
    return [
        (result[i * N : (i + 1) * N, :N], result[i * N : (i + 1) * N, N:])
        for i in range(len(pairs))
    ]


def forward(signals, first, high, low, cos, sin):
    signal_high, signal_low = split(jnp.concatenate(signals, axis=1))
    mixed = dot(first, jnp.concatenate([signal_high, signal_high, signal_low], axis=0))
    pairs = []
    for i in range(len(signals)):
        re, im = columns(mixed[:N], i), columns(mixed[N:], i)
        pairs.append((re * cos + im * sin, im * cos - re * sin))
    return by_inner(pairs, high, low)


def inverse(spectra, last, high, low, cos, sin):
    turned_re, turned_im = [], []
    for re, im in by_inner(spectra, high, low):
        turned_re.append(re * cos - im * sin)
        turned_im.append(re * sin + im * cos)
    stacked = jnp.concatenate(
        [jnp.concatenate(turned_re, axis=1), jnp.concatenate(turned_im, axis=1)], axis=0
    )
    stacked_high, stacked_low = split(stacked)
    return dot(last, jnp.concatenate([stacked_high, stacked_high, stacked_low], axis=0))


def times(a, b):
    return (a[0] * b[0] - a[1] * b[1], a[0] * b[1] + a[1] * b[0])


def conj_times(a, b):
    return (a[0] * b[0] + a[1] * b[1], a[0] * b[1] - a[1] * b[0])


def exchange_kernel(
    size,
    q_hbm, k_hbm, v_hbm, c_hbm, filt_hbm, first_hbm, last_hbm, middle_hbm, turn_hbm,
    back_ref, own_ref, other_ref, q_ref, k_ref, v_ref, c_ref,
    filt_ref, first_f32, last_f32, middle_f32, turn_ref,
    first_ref, last_ref, middle_ref, send_ref, recv_ref, out_ref, spec_ref,
    load_sems, in_send, in_recv, out_send, out_recv, pair_send, pair_recv,
):
    me = lax.axis_index("context")
    pair = lax.axis_index("dp")

    def around(index):
        return jnp.where(index >= size, index - size, index)

    def loader(i, source, target):
        return pltpu.make_async_copy(source, target, load_sems.at[i])

    loads = [
        loader(i, source, target)
        for i, (source, target) in enumerate(
            [
                (k_hbm, k_ref), (v_hbm, v_ref), (c_hbm, c_ref), (q_hbm, q_ref),
                (filt_hbm, filt_ref), (first_hbm, first_f32), (last_hbm, last_f32),
                (middle_hbm, middle_f32), (turn_hbm, turn_ref),
            ]
        )
    ]
    for load in loads:
        load.start()

    barrier = pltpu.get_barrier_semaphore()

    @pl.loop(1, size, unroll=8)
    def _(step):
        pl.semaphore_signal(
            barrier, inc=1, device_id=(pair, around(me + step)), device_id_type=MESH
        )

    pl.semaphore_signal(barrier, inc=1, device_id=(1 - pair, me), device_id_type=MESH)

    for load in loads[:4]:
        load.wait()

    def rows_of(peer):
        return pl.ds(pl.multiple_of(peer * ROWS, ROWS), ROWS)

    def products(chunk):
        @pl.loop(0, size, unroll=8)
        def _(peer):
            base = pl.multiple_of(peer * ROWS, ROWS)
            send_ref[chunk, pl.ds(base, SUB), :] = k_ref[peer, chunk] * v_ref[peer, chunk]
            send_ref[chunk, pl.ds(base + SUB, SUB), :] = c_ref[peer, chunk] * q_ref[peer, chunk]

    def send_all(chunk, source, target, send_sem, recv_sem):
        target[chunk, rows_of(me), :] = source[chunk, rows_of(me), :]

        @pl.loop(1, size)
        def _(step):
            peer = around(me + step)
            pltpu.make_async_remote_copy(
                src_ref=source.at[chunk, rows_of(peer), :],
                dst_ref=target.at[chunk, rows_of(me), :],
                send_sem=send_sem.at[chunk],
                recv_sem=recv_sem.at[chunk],
                device_id=(pair, peer),
                device_id_type=MESH,
            ).start()

    def await_all(chunk, ref, sem):
        part = ref.at[chunk, pl.ds(0, (size - 1) * ROWS), :]
        pltpu.make_async_copy(part, part, sem.at[chunk]).wait()

    products(0)
    pl.semaphore_wait(barrier, size)
    send_all(0, send_ref, recv_ref, in_send, in_recv)
    products(1)
    send_all(1, send_ref, recv_ref, in_send, in_recv)

    for load in loads[4:]:
        load.wait()

    def thirds(table):
        high, low = split(table)
        return jnp.concatenate([high, low, high], axis=1)

    first_ref[...] = thirds(first_f32[...])
    last_ref[...] = thirds(last_f32[...])
    for way in range(2):
        middle_ref[2 * way], middle_ref[2 * way + 1] = split(middle_f32[way])

    def ahead(signals):
        return forward(
            signals, first_ref[...], middle_ref[0], middle_ref[1], turn_ref[0], turn_ref[1]
        )

    for chunk in range(CHUNKS):
        @pl.loop(0, SUB // 4)
        def _(step):
            at = step * 4
            signals = [filt_ref[chunk, pl.ds(at + i, N, stride=SUB), :] for i in range(4)]
            for i, (re, im) in enumerate(ahead(signals)):
                spec_ref[chunk, at + i, 0] = re
                spec_ref[chunk, at + i, 1] = im

    def convolve(chunk):
        @pl.loop(0, SUB // 2)
        def _(step):
            at = step * 2
            signals = [
                recv_ref[chunk, pl.ds(at + i + SUB * signal, N, stride=ROWS), :]
                for i in range(2)
                for signal in range(2)
            ]
            spectra = ahead(signals)
            mixed = []
            for i in range(2):
                product, grad = spectra[2 * i], spectra[2 * i + 1]
                filt = (spec_ref[chunk, at + i, 0], spec_ref[chunk, at + i, 1])
                mixed.append(times(filt, product))
                mixed.append(conj_times(filt, grad))
                mixed.append(conj_times(product, grad))
            results = inverse(
                mixed, last_ref[...], middle_ref[2], middle_ref[3], turn_ref[0], turn_ref[1]
            )
            for i in range(2):
                out_ref[chunk, pl.ds(at + i, N, stride=ROWS), :] = columns(results, 3 * i)
                out_ref[chunk, pl.ds(at + i + SUB, N, stride=ROWS), :] = columns(
                    results, 3 * i + 1
                )
                own_ref[chunk, pl.ds(at + i, N, stride=SUB), :] = columns(results, 3 * i + 2)

    def pair_copy(chunk):
        return pltpu.make_async_remote_copy(
            src_ref=own_ref.at[chunk],
            dst_ref=other_ref.at[chunk],
            send_sem=pair_send.at[chunk],
            recv_sem=pair_recv.at[chunk],
            device_id=(1 - pair, me),
            device_id_type=MESH,
        )

    for chunk in range(CHUNKS):
        await_all(chunk, recv_ref, in_recv)
        convolve(chunk)
        send_all(chunk, out_ref, back_ref, out_send, out_recv)
        pair_copy(chunk).start()

    for chunk in range(CHUNKS):
        pair_copy(chunk).wait()
        await_all(chunk, send_ref, in_send)
        await_all(chunk, out_ref, out_send)
    for chunk in range(CHUNKS):
        await_all(chunk, back_ref, out_recv)


def gate_kernel(
    scale, pieces,
    q_ref, k_ref, v_ref, c_ref, back_ref, own_ref, other_ref,
    gated_hbm, grad_q_hbm, grad_k_hbm, grad_v_hbm, grad_f_hbm,
    gated_ref, grad_q_ref, grad_k_ref, grad_v_ref, grad_f_ref, sems,
):
    block = q_ref.shape[0] // pieces
    stores = []

    def store(source, target):
        copy = pltpu.make_async_copy(source, target, sems.at[len(stores)])
        copy.start()
        stores.append(copy)

    for piece in range(pieces):
        @pl.loop(piece * block, (piece + 1) * block, unroll=4)
        def _(peer):
            base = pl.multiple_of(peer * ROWS, ROWS)
            for chunk in range(CHUNKS):
                conv = back_ref[chunk, pl.ds(base, SUB), :]
                back = back_ref[chunk, pl.ds(base + SUB, SUB), :]
                gated_ref[peer, chunk] = q_ref[peer, chunk] * conv
                grad_q_ref[peer, chunk] = c_ref[peer, chunk] * conv
                grad_k_ref[peer, chunk] = v_ref[peer, chunk] * back
                grad_v_ref[peer, chunk] = k_ref[peer, chunk] * back
                rows = pl.ds(pl.multiple_of(peer * SUB, SUB), SUB)
                grad_f_ref[chunk, rows, :] = (
                    own_ref[chunk, rows, :] + other_ref[chunk, rows, :]
                ) * scale

        part = pl.ds(piece * block, block)
        for source, target in (
            (gated_ref, gated_hbm), (grad_q_ref, grad_q_hbm),
            (grad_k_ref, grad_k_hbm), (grad_v_ref, grad_v_hbm),
        ):
            store(source.at[part], target.at[part])
        rows = pl.ds(piece * block * SUB, block * SUB)
        for chunk in range(CHUNKS):
            store(grad_f_ref.at[chunk, rows, :], grad_f_hbm.at[chunk, rows, :])
    for copy in stores:
        copy.wait()


def on_device(query_input, key_input, value_input, filters, cotangent):
    size = lax.axis_size("context")
    channels = query_input.shape[1]
    rows, length = filters.shape
    scale = 1.0 / math.sqrt(lax.axis_size("dp") * length)
    token_shape = (size, CHUNKS, SUB, LANES)
    tokens = [
        array.reshape(token_shape) for array in (query_input, key_input, value_input, cotangent)
    ]
    taps = filters.reshape(CHUNKS, SUB, size, LANES).transpose(0, 2, 1, 3)
    taps = taps.reshape(CHUNKS, size * SUB, LANES)
    constants = [jnp.asarray(table) for table in tables()]

    hbm_spec = pl.BlockSpec(memory_space=pltpu.HBM)
    vmem_spec = pl.BlockSpec(memory_space=pltpu.VMEM)
    wide = (CHUNKS, size * ROWS, LANES)
    narrow = (CHUNKS, size * SUB, LANES)
    token_out = jax.ShapeDtypeStruct(token_shape, F32)
    narrow_out = jax.ShapeDtypeStruct(narrow, F32)
    per_chunk = pltpu.SemaphoreType.DMA((CHUNKS,))
    def pinned(array):
        return pltpu.with_memory_space_constraint(array, pltpu.HBM)

    back, own, other, *held = pl.pallas_call(
        functools.partial(exchange_kernel, size),
        out_shape=[pltpu.VMEM(shape, F32) for shape in [wide, narrow, narrow] + [token_shape] * 4],
        in_specs=[hbm_spec] * 9,
        out_specs=[vmem_spec] * 7,
        scratch_shapes=[pltpu.VMEM(narrow, F32)]
        + [pltpu.VMEM(table.shape, table.dtype) for table in constants]
        + [
            pltpu.VMEM((2 * N, 3 * N), BF16),
            pltpu.VMEM((N, 6 * N), BF16),
            pltpu.VMEM((4, 2 * N, 2 * N), BF16),
            pltpu.VMEM(wide, F32),
            pltpu.VMEM(wide, F32),
            pltpu.VMEM(wide, F32),
            pltpu.VMEM((CHUNKS, SUB, 2, N, LANES), F32),
            pltpu.SemaphoreType.DMA((9,)),
        ]
        + [per_chunk] * 6,
        compiler_params=pltpu.CompilerParams(
            collective_id=0, has_side_effects=True, vmem_limit_bytes=40 * 2**20
        ),
        name="exchange",
    )(*map(pinned, (*tokens, taps, *constants)))

    pieces = 4
    results = pl.pallas_call(
        functools.partial(gate_kernel, scale, pieces),
        out_shape=[token_out] * 4 + [narrow_out],
        in_specs=[vmem_spec] * 7,
        out_specs=[hbm_spec] * 5,
        scratch_shapes=[pltpu.VMEM(token_shape, F32) for _ in range(4)]
        + [pltpu.VMEM(narrow, F32), pltpu.SemaphoreType.DMA((pieces * (4 + CHUNKS),))],
        compiler_params=pltpu.CompilerParams(vmem_limit_bytes=20 * 2**20),
        name="gate",
    )(*held, back, own, other)
    per_token = [array.reshape(1, channels, LANES) for array in results[:4]]
    grad_filter = results[4].reshape(CHUNKS, size, SUB, LANES).transpose(0, 2, 1, 3)
    return (*per_token, grad_filter.reshape(rows, length))


def solution(mesh):
    token = P("dp", None, "context")
    taps = P("context", None)
    return jax.shard_map(
        on_device,
        mesh=mesh,
        in_specs=(token, token, token, taps, token),
        out_specs=(token, token, token, token, taps),
        check_vma=False,
    )
```

```python
import functools
import math

import jax
import jax.numpy as jnp
import numpy as np
from jax import lax
from jax.experimental import pallas as pl
from jax.experimental.pallas import tpu as pltpu
from jax.sharding import PartitionSpec as P

MESH = pl.DeviceIdType.MESH
F32 = jnp.float32
BF16 = jnp.bfloat16
N = 128
SUB = 8
CHUNKS = 2
ROWS = 2 * SUB
LANES = 128
STRIDE, LINE = 4, 8


def tables():
    steps = np.arange(N, dtype=np.float64)
    total = N * N
    outer = 2.0 * math.pi / N * (steps[:, None] + 0.25) * steps[None, :]
    twist = 2.0 * math.pi / total * (steps[:, None] + 0.25) * steps[None, :]
    inner = 2.0 * math.pi / N * ((steps[:, None] * steps[None, :]) % N)
    first = np.concatenate([np.cos(outer), -np.sin(outer)], axis=0)
    last = np.concatenate([np.cos(outer.T), -np.sin(outer.T)], axis=1) / total
    cos, sin = np.cos(inner), np.sin(inner)
    middle = np.stack([np.block([[cos, -sin], [sin, cos]]), np.block([[cos, sin], [-sin, cos]])])
    turn = np.stack([np.cos(twist), np.sin(twist)])
    return [table.astype(np.float32) for table in (first, last, middle, turn)]


def split(value):
    high = value.astype(BF16)
    low = (value - high.astype(F32)).astype(BF16)
    return high, low


def dot(left, right):
    return jnp.dot(left, right, preferred_element_type=F32)


def columns(value, index):
    return value[:, index * LANES : (index + 1) * LANES]


def by_inner(pairs, high, low):
    stacked = jnp.concatenate([jnp.concatenate(pair, axis=1) for pair in pairs], axis=0)
    stacked_high, stacked_low = split(stacked)
    result = dot(stacked_high, high) + dot(stacked_low, high) + dot(stacked_high, low)
    return [
        (result[i * N : (i + 1) * N, :N], result[i * N : (i + 1) * N, N:])
        for i in range(len(pairs))
    ]


def forward(signals, first, high, low, cos, sin):
    signal_high, signal_low = split(jnp.concatenate(signals, axis=1))
    mixed = dot(first, jnp.concatenate([signal_high, signal_high, signal_low], axis=0))
    pairs = []
    for i in range(len(signals)):
        re, im = columns(mixed[:N], i), columns(mixed[N:], i)
        pairs.append((re * cos + im * sin, im * cos - re * sin))
    return by_inner(pairs, high, low)


def inverse(spectra, last, high, low, cos, sin):
    turned_re, turned_im = [], []
    for re, im in by_inner(spectra, high, low):
        turned_re.append(re * cos - im * sin)
        turned_im.append(re * sin + im * cos)
    stacked = jnp.concatenate(
        [jnp.concatenate(turned_re, axis=1), jnp.concatenate(turned_im, axis=1)], axis=0
    )
    stacked_high, stacked_low = split(stacked)
    return dot(last, jnp.concatenate([stacked_high, stacked_high, stacked_low], axis=0))


def times(a, b):
    return (a[0] * b[0] - a[1] * b[1], a[0] * b[1] + a[1] * b[0])


def conj_times(a, b):
    return (a[0] * b[0] + a[1] * b[1], a[0] * b[1] - a[1] * b[0])


def gate(chunk, peer, factors, back_ref, results):
    base = pl.multiple_of(peer * ROWS, ROWS)
    conv = back_ref[chunk, pl.ds(base, SUB), :]
    back = back_ref[chunk, pl.ds(base + SUB, SUB), :]
    for factor, signal, result in zip(factors, (conv, conv, back, back), results):
        result[peer] = factor[peer, chunk] * signal


def exchange_kernel(
    size, scale,
    q_hbm, k_hbm, v_hbm, c_hbm, filt_hbm, first_hbm, last_hbm, middle_hbm, turn_hbm,
    back_ref, grad_f_ref, gated_ref, grad_q_ref, grad_k_ref, grad_v_ref,
    q_ref, k_ref, v_ref, c_ref,
    own_ref, other_ref, filt_ref, first_f32, last_f32, middle_f32, turn_ref,
    first_ref, last_ref, middle_ref, send_ref, recv_ref, out_ref, spec_ref,
    load_sems, wave_sem, in_send, in_recv, out_send, out_recv, pair_send, pair_recv,
):
    me = lax.axis_index("context")
    pair = lax.axis_index("dp")

    planes = size // LINE
    place = lax.rem(me // STRIDE, LINE)
    spot = me // (STRIDE * LINE) * STRIDE + lax.rem(me, STRIDE)

    def peer_at(line, plane):
        z = place + line
        z = jnp.where(z >= LINE, z - LINE, z)
        at = spot + plane
        at = jnp.where(at >= planes, at - planes, at)
        return (at // STRIDE * LINE + z) * STRIDE + lax.rem(at, STRIDE)

    def loader(i, source, target):
        return pltpu.make_async_copy(source, target, load_sems.at[i])

    loads = [
        loader(i, source, target)
        for i, (source, target) in enumerate(
            [
                (source.at[:, chunk], target.at[:, chunk])
                for chunk in range(CHUNKS)
                for source, target in (
                    (k_hbm, k_ref), (v_hbm, v_ref), (c_hbm, c_ref), (q_hbm, q_ref)
                )
            ]
            + [
                (filt_hbm, filt_ref), (first_hbm, first_f32), (last_hbm, last_f32),
                (middle_hbm, middle_f32), (turn_hbm, turn_ref),
            ]
        )
    ]
    for load in loads[:4]:
        load.start()

    barrier = pltpu.get_barrier_semaphore()

    def greet(semaphore, peer):
        pl.semaphore_signal(semaphore, inc=1, device_id=(pair, peer), device_id_type=MESH)

    for plane in range(1, planes):
        greet(barrier, peer_at(0, plane))
    for line in (1, LINE - 1):
        greet(barrier, peer_at(line, 0))
    pl.semaphore_signal(barrier, inc=1, device_id=(1 - pair, me), device_id_type=MESH)
    for load in loads[4:]:
        load.start()

    def tell(stage):
        for line in (1, LINE - 1):
            greet(wave_sem.at[stage], peer_at(line, 0))

    pl.semaphore_wait(barrier, planes + 2)
    tell(0)
    for load in loads[:4]:
        load.wait()

    def rows_of(peer):
        return pl.ds(pl.multiple_of(peer * ROWS, ROWS), ROWS)

    def products(chunk):
        @pl.loop(0, size, unroll=8)
        def _(peer):
            base = pl.multiple_of(peer * ROWS, ROWS)
            send_ref[chunk, pl.ds(base, SUB), :] = k_ref[peer, chunk] * v_ref[peer, chunk]
            send_ref[chunk, pl.ds(base + SUB, SUB), :] = c_ref[peer, chunk] * q_ref[peer, chunk]

    def sender(chunk, source, target, send_sem, recv_sem):
        def send(line, plane):
            peer = peer_at(line, plane)
            pltpu.make_async_remote_copy(
                src_ref=source.at[chunk, rows_of(peer), :],
                dst_ref=target.at[chunk, rows_of(me), :],
                send_sem=send_sem.at[chunk],
                recv_sem=recv_sem.at[chunk],
                device_id=(pair, peer),
                device_id_type=MESH,
            ).start()

        return send

    def keep(chunk, source, target):
        target[chunk, rows_of(me), :] = source[chunk, rows_of(me), :]

    def send_plane(send, line):
        @pl.loop(0, planes)
        def _(plane):
            send(line, plane)

    def send_own_plane(send):
        @pl.loop(1, planes)
        def _(plane):
            send(0, plane)

    def send_all(chunk, source, target, send_sem, recv_sem):
        keep(chunk, source, target)
        send = sender(chunk, source, target, send_sem, recv_sem)
        for line in (4, 1, 7, 2, 6, 3, 5):
            send(line, 0)

        @pl.loop(1, planes)
        def _(plane):
            for line in (4, 1, 7, 2, 0, 6, 3, 5):
                send(line, plane)

    def await_all(chunk, ref, sem):
        part = ref.at[chunk, pl.ds(0, (size - 1) * ROWS), :]
        pltpu.make_async_copy(part, part, sem.at[chunk]).wait()

    products(0)
    keep(0, send_ref, recv_ref)
    send = sender(0, send_ref, recv_ref, in_send, in_recv)
    for stage in range(1, LINE // 2):
        pl.semaphore_wait(wave_sem.at[stage - 1], 2)
        tell(stage)
        send_plane(send, stage)
        send_plane(send, LINE - stage)
    pl.semaphore_wait(wave_sem.at[LINE // 2 - 1], 2)
    send_plane(send, LINE // 2)
    send_own_plane(send)
    for load in loads[4:8]:
        load.wait()
    products(1)
    send_all(1, send_ref, recv_ref, in_send, in_recv)

    for load in loads[8:]:
        load.wait()

    def thirds(table):
        high, low = split(table)
        return jnp.concatenate([high, low, high], axis=1)

    first_ref[...] = thirds(first_f32[...])
    last_ref[...] = thirds(last_f32[...])
    for way in range(2):
        middle_ref[2 * way], middle_ref[2 * way + 1] = split(middle_f32[way])

    def ahead(signals):
        return forward(
            signals, first_ref[...], middle_ref[0], middle_ref[1], turn_ref[0], turn_ref[1]
        )

    for chunk in range(CHUNKS):
        @pl.loop(0, SUB // 4)
        def _(step):
            at = step * 4
            signals = [filt_ref[chunk, pl.ds(at + i, N, stride=SUB), :] for i in range(4)]
            for i, (re, im) in enumerate(ahead(signals)):
                spec_ref[chunk, at + i, 0] = re
                spec_ref[chunk, at + i, 1] = im

    def convolve(chunk):
        @pl.loop(0, SUB // 2)
        def _(step):
            at = step * 2
            signals = [
                recv_ref[chunk, pl.ds(at + i + SUB * signal, N, stride=ROWS), :]
                for i in range(2)
                for signal in range(2)
            ]
            spectra = ahead(signals)
            mixed = []
            for i in range(2):
                product, grad = spectra[2 * i], spectra[2 * i + 1]
                filt = (spec_ref[chunk, at + i, 0], spec_ref[chunk, at + i, 1])
                mixed.append(times(filt, product))
                mixed.append(conj_times(filt, grad))
                mixed.append(conj_times(product, grad))
            results = inverse(
                mixed, last_ref[...], middle_ref[2], middle_ref[3], turn_ref[0], turn_ref[1]
            )
            for i in range(2):
                out_ref[chunk, pl.ds(at + i, N, stride=ROWS), :] = columns(results, 3 * i)
                out_ref[chunk, pl.ds(at + i + SUB, N, stride=ROWS), :] = columns(
                    results, 3 * i + 1
                )
                own_ref[chunk, pl.ds(at + i, N, stride=SUB), :] = columns(results, 3 * i + 2)

    def pair_copy(chunk):
        return pltpu.make_async_remote_copy(
            src_ref=own_ref.at[chunk],
            dst_ref=other_ref.at[chunk],
            send_sem=pair_send.at[chunk],
            recv_sem=pair_recv.at[chunk],
            device_id=(1 - pair, me),
            device_id_type=MESH,
        )

    for chunk in range(CHUNKS):
        await_all(chunk, recv_ref, in_recv)
        convolve(chunk)
        send_all(chunk, out_ref, back_ref, out_send, out_recv)
        pair_copy(chunk).start()

    for chunk in range(CHUNKS):
        pair_copy(chunk).wait()
    grad_f_ref[...] = (own_ref[...] + other_ref[...]) * scale

    await_all(0, back_ref, out_recv)
    results = (gated_ref, grad_q_ref, grad_k_ref, grad_v_ref)

    @pl.loop(0, size, unroll=4)
    def _(peer):
        gate(0, peer, (q_ref, c_ref, v_ref, k_ref), back_ref, results)

    for chunk in range(CHUNKS):
        await_all(chunk, send_ref, in_send)
        await_all(chunk, out_ref, out_send)
    await_all(1, back_ref, out_recv)


def store_kernel(
    pieces,
    back_ref, grad_f_ref, gated_ref, grad_q_ref, grad_k_ref, grad_v_ref,
    q_ref, k_ref, v_ref, c_ref,
    gated_hbm, grad_q_hbm, grad_k_hbm, grad_v_hbm, grad_f_hbm,
    late_gated, late_grad_q, late_grad_k, late_grad_v, sems,
):
    block = q_ref.shape[0] // pieces
    early = (gated_ref, grad_q_ref, grad_k_ref, grad_v_ref)
    late = (late_gated, late_grad_q, late_grad_k, late_grad_v)
    targets = (gated_hbm, grad_q_hbm, grad_k_hbm, grad_v_hbm)
    stores = []

    def store(source, target):
        copy = pltpu.make_async_copy(source, target, sems.at[len(stores)])
        copy.start()
        stores.append(copy)

    for source, target in zip(early, targets):
        store(source, target.at[:, 0])
    store(grad_f_ref, grad_f_hbm)
    for piece in range(pieces):
        @pl.loop(piece * block, (piece + 1) * block, unroll=4)
        def _(peer):
            gate(1, peer, (q_ref, c_ref, v_ref, k_ref), back_ref, late)

        part = pl.ds(piece * block, block)
        for source, target in zip(late, targets):
            store(source.at[part], target.at[part, 1])
    for copy in stores:
        copy.wait()


def on_device(query_input, key_input, value_input, filters, cotangent):
    size = lax.axis_size("context")
    channels = query_input.shape[1]
    rows, length = filters.shape
    scale = 1.0 / math.sqrt(lax.axis_size("dp") * length)
    token_shape = (size, CHUNKS, SUB, LANES)
    tokens = [
        array.reshape(token_shape) for array in (query_input, key_input, value_input, cotangent)
    ]
    taps = filters.reshape(CHUNKS, SUB, size, LANES).transpose(0, 2, 1, 3)
    taps = taps.reshape(CHUNKS, size * SUB, LANES)
    constants = [jnp.asarray(table) for table in tables()]

    hbm_spec = pl.BlockSpec(memory_space=pltpu.HBM)
    vmem_spec = pl.BlockSpec(memory_space=pltpu.VMEM)
    wide = (CHUNKS, size * ROWS, LANES)
    narrow = (CHUNKS, size * SUB, LANES)
    half = (size, SUB, LANES)
    per_chunk = pltpu.SemaphoreType.DMA((CHUNKS,))
    def pinned(array):
        return pltpu.with_memory_space_constraint(array, pltpu.HBM)

    held = pl.pallas_call(
        functools.partial(exchange_kernel, size, scale),
        out_shape=[
            pltpu.VMEM(shape, F32) for shape in [wide, narrow] + [half] * 4 + [token_shape] * 4
        ],
        in_specs=[hbm_spec] * 9,
        out_specs=[vmem_spec] * 10,
        scratch_shapes=[pltpu.VMEM(narrow, F32) for _ in range(3)]
        + [pltpu.VMEM(table.shape, table.dtype) for table in constants]
        + [
            pltpu.VMEM((2 * N, 3 * N), BF16),
            pltpu.VMEM((N, 6 * N), BF16),
            pltpu.VMEM((4, 2 * N, 2 * N), BF16),
            pltpu.VMEM(wide, F32),
            pltpu.VMEM(wide, F32),
            pltpu.VMEM(wide, F32),
            pltpu.VMEM((CHUNKS, SUB, 2, N, LANES), F32),
            pltpu.SemaphoreType.DMA((4 * CHUNKS + 5,)),
            pltpu.SemaphoreType.REGULAR((LINE // 2,)),
        ]
        + [per_chunk] * 6,
        compiler_params=pltpu.CompilerParams(
            collective_id=0, has_side_effects=True, vmem_limit_bytes=40 * 2**20
        ),
        name="exchange",
    )(*map(pinned, (*tokens, taps, *constants)))

    pieces = 2
    results = pl.pallas_call(
        functools.partial(store_kernel, pieces),
        out_shape=[jax.ShapeDtypeStruct(token_shape, F32)] * 4
        + [jax.ShapeDtypeStruct(narrow, F32)],
        in_specs=[vmem_spec] * 10,
        out_specs=[hbm_spec] * 5,
        scratch_shapes=[pltpu.VMEM(half, F32) for _ in range(4)]
        + [pltpu.SemaphoreType.DMA((5 + 4 * pieces,))],
        compiler_params=pltpu.CompilerParams(vmem_limit_bytes=20 * 2**20),
        name="store",
    )(*held)
    per_token = [array.reshape(1, channels, LANES) for array in results[:4]]
    grad_filter = results[4].reshape(CHUNKS, size, SUB, LANES).transpose(0, 2, 1, 3)
    return (*per_token, grad_filter.reshape(rows, length))


def solution(mesh):
    token = P("dp", None, "context")
    taps = P("context", None)
    return jax.shard_map(
        on_device,
        mesh=mesh,
        in_specs=(token, token, token, taps, token),
        out_specs=(token, token, token, token, taps),
        check_vma=False,
    )
```

```python
import functools
import math

import jax
import jax.numpy as jnp
import numpy as np
from jax import lax
from jax.experimental import pallas as pl
from jax.experimental.pallas import tpu as pltpu
from jax.sharding import PartitionSpec as P

MESH = pl.DeviceIdType.MESH
F32 = jnp.float32
BF16 = jnp.bfloat16
N = 128
SUB = 8
CHUNKS = 2
ROWS = 2 * SUB
LANES = 128
STRIDE, LINE = 4, 8


def tables():
    steps = np.arange(N, dtype=np.float64)
    total = N * N
    outer = 2.0 * math.pi / N * (steps[:, None] + 0.25) * steps[None, :]
    twist = 2.0 * math.pi / total * (steps[:, None] + 0.25) * steps[None, :]
    inner = 2.0 * math.pi / N * ((steps[:, None] * steps[None, :]) % N)
    first = np.concatenate([np.cos(outer), -np.sin(outer)], axis=0)
    last = np.concatenate([np.cos(outer.T), -np.sin(outer.T)], axis=1) / total
    cos, sin = np.cos(inner), np.sin(inner)
    middle = np.stack([np.block([[cos, -sin], [sin, cos]]), np.block([[cos, sin], [-sin, cos]])])
    turn = np.stack([np.cos(twist), np.sin(twist)])
    return [table.astype(np.float32) for table in (first, last, middle, turn)]


def split(value):
    high = value.astype(BF16)
    low = (value - high.astype(F32)).astype(BF16)
    return high, low


def dot(left, right):
    return jnp.dot(left, right, preferred_element_type=F32)


def columns(value, index):
    return value[:, index * LANES : (index + 1) * LANES]


def by_inner(pairs, high, low):
    stacked = jnp.concatenate([jnp.concatenate(pair, axis=1) for pair in pairs], axis=0)
    stacked_high, stacked_low = split(stacked)
    result = dot(stacked_high, high) + dot(stacked_low, high) + dot(stacked_high, low)
    return [
        (result[i * N : (i + 1) * N, :N], result[i * N : (i + 1) * N, N:])
        for i in range(len(pairs))
    ]


def forward(signals, first, high, low, cos, sin):
    signal_high, signal_low = split(jnp.concatenate(signals, axis=1))
    mixed = dot(first, jnp.concatenate([signal_high, signal_high, signal_low], axis=0))
    pairs = []
    for i in range(len(signals)):
        re, im = columns(mixed[:N], i), columns(mixed[N:], i)
        pairs.append((re * cos + im * sin, im * cos - re * sin))
    return by_inner(pairs, high, low)


def inverse(spectra, last, high, low, cos, sin):
    turned_re, turned_im = [], []
    for re, im in by_inner(spectra, high, low):
        turned_re.append(re * cos - im * sin)
        turned_im.append(re * sin + im * cos)
    stacked = jnp.concatenate(
        [jnp.concatenate(turned_re, axis=1), jnp.concatenate(turned_im, axis=1)], axis=0
    )
    stacked_high, stacked_low = split(stacked)
    return dot(last, jnp.concatenate([stacked_high, stacked_high, stacked_low], axis=0))


def times(a, b):
    return (a[0] * b[0] - a[1] * b[1], a[0] * b[1] + a[1] * b[0])


def conj_times(a, b):
    return (a[0] * b[0] + a[1] * b[1], a[0] * b[1] - a[1] * b[0])


def gate(chunk, peer, factors, back_ref, results):
    base = pl.multiple_of(peer * ROWS, ROWS)
    conv = back_ref[chunk, pl.ds(base, SUB), :]
    back = back_ref[chunk, pl.ds(base + SUB, SUB), :]
    for factor, signal, result in zip(factors, (conv, conv, back, back), results):
        result[peer] = factor[peer, chunk] * signal


def exchange_kernel(
    size, scale,
    q_hbm, k_hbm, v_hbm, c_hbm, filt_hbm, first_hbm, last_hbm, middle_hbm, turn_hbm,
    back_ref, grad_f_ref, gated_ref, grad_q_ref, grad_k_ref, grad_v_ref,
    q_ref, k_ref, v_ref, c_ref,
    own_ref, other_ref, filt_ref, first_f32, last_f32, middle_f32, turn_ref,
    first_ref, last_ref, middle_ref, send_ref, recv_ref, out_ref, spec_ref,
    load_sems, wave_sem, in_send, in_recv, out_send, out_recv, pair_send, pair_recv,
):
    me = lax.axis_index("context")
    pair = lax.axis_index("dp")
    taps = pl.ds(0, size * SUB)

    planes = size // LINE
    place = lax.rem(me // STRIDE, LINE)
    spot = me // (STRIDE * LINE) * STRIDE + lax.rem(me, STRIDE)

    def peer_at(line, plane):
        z = place + line
        z = jnp.where(z >= LINE, z - LINE, z)
        at = spot + plane
        at = jnp.where(at >= planes, at - planes, at)
        return (at // STRIDE * LINE + z) * STRIDE + lax.rem(at, STRIDE)

    def loader(i, source, target):
        return pltpu.make_async_copy(source, target, load_sems.at[i])

    loads = [
        loader(i, source, target)
        for i, (source, target) in enumerate(
            [
                (source.at[:, chunk], target.at[:, chunk])
                for chunk in range(CHUNKS)
                for source, target in (
                    (k_hbm, k_ref), (v_hbm, v_ref), (c_hbm, c_ref), (q_hbm, q_ref)
                )
            ]
            + [
                (filt_hbm, filt_ref.at[:, taps, :]), (first_hbm, first_f32), (last_hbm, last_f32),
                (middle_hbm, middle_f32), (turn_hbm, turn_ref),
            ]
        )
    ]
    for load in loads[:4]:
        load.start()

    barrier = pltpu.get_barrier_semaphore()

    def greet(semaphore, peer):
        pl.semaphore_signal(semaphore, inc=1, device_id=(pair, peer), device_id_type=MESH)

    for plane in range(1, planes):
        greet(barrier, peer_at(0, plane))
    for line in (1, LINE - 1):
        greet(barrier, peer_at(line, 0))
    pl.semaphore_signal(barrier, inc=1, device_id=(1 - pair, me), device_id_type=MESH)
    for load in loads[4:]:
        load.start()

    def tell(stage):
        for line in (1, LINE - 1):
            greet(wave_sem.at[stage], peer_at(line, 0))

    pl.semaphore_wait(barrier, planes + 2)
    tell(0)
    for load in loads[:4]:
        load.wait()

    def rows_of(peer):
        return pl.ds(pl.multiple_of(peer * ROWS, ROWS), ROWS)

    def products(chunk):
        @pl.loop(0, size, unroll=8)
        def _(peer):
            base = pl.multiple_of(peer * ROWS, ROWS)
            send_ref[chunk, pl.ds(base, SUB), :] = k_ref[peer, chunk] * v_ref[peer, chunk]
            send_ref[chunk, pl.ds(base + SUB, SUB), :] = c_ref[peer, chunk] * q_ref[peer, chunk]

    def sender(chunk, source, target, send_sem, recv_sem):
        def send(line, plane):
            peer = peer_at(line, plane)
            pltpu.make_async_remote_copy(
                src_ref=source.at[chunk, rows_of(peer), :],
                dst_ref=target.at[chunk, rows_of(me), :],
                send_sem=send_sem.at[chunk],
                recv_sem=recv_sem.at[chunk],
                device_id=(pair, peer),
                device_id_type=MESH,
            ).start()

        return send

    def keep(chunk, source, target):
        target[chunk, rows_of(me), :] = source[chunk, rows_of(me), :]

    def send_plane(send, line):
        @pl.loop(0, planes)
        def _(plane):
            send(line, plane)

    def send_own_plane(send):
        @pl.loop(1, planes)
        def _(plane):
            send(0, plane)

    def send_all(chunk, source, target, send_sem, recv_sem):
        keep(chunk, source, target)
        send = sender(chunk, source, target, send_sem, recv_sem)
        for line in (4, 1, 7, 2, 6, 3, 5):
            send(line, 0)

        @pl.loop(1, planes)
        def _(plane):
            for line in (4, 1, 7, 2, 0, 6, 3, 5):
                send(line, plane)

    def await_all(chunk, ref, sem):
        part = ref.at[chunk, pl.ds(0, (size - 1) * ROWS), :]
        pltpu.make_async_copy(part, part, sem.at[chunk]).wait()

    products(0)
    keep(0, send_ref, recv_ref)
    send = sender(0, send_ref, recv_ref, in_send, in_recv)
    for stage in range(1, LINE // 2):
        pl.semaphore_wait(wave_sem.at[stage - 1], 2)
        tell(stage)
        send_plane(send, stage)
        send_plane(send, LINE - stage)
    pl.semaphore_wait(wave_sem.at[LINE // 2 - 1], 2)
    send_plane(send, LINE // 2)
    send_own_plane(send)
    for load in loads[4:8]:
        load.wait()
    products(1)
    send_all(1, send_ref, recv_ref, in_send, in_recv)

    for load in loads[8:]:
        load.wait()

    def thirds(table):
        high, low = split(table)
        return jnp.concatenate([high, low, high], axis=1)

    first_ref[...] = thirds(first_f32[...])
    last_ref[...] = thirds(last_f32[...])
    for way in range(2):
        middle_ref[2 * way], middle_ref[2 * way + 1] = split(middle_f32[way])

    def ahead(signals):
        return forward(
            signals, first_ref[...], middle_ref[0], middle_ref[1], turn_ref[0], turn_ref[1]
        )

    for chunk in range(CHUNKS):
        @pl.loop(0, SUB // 4)
        def _(step):
            at = step * 4
            signals = [filt_ref[chunk, pl.ds(at + i, N, stride=SUB), :] for i in range(4)]
            for i, (re, im) in enumerate(ahead(signals)):
                spec_ref[chunk, at + i, 0] = re
                spec_ref[chunk, at + i, 1] = im

    def convolve(chunk):
        @pl.loop(0, SUB // 2)
        def _(step):
            at = step * 2
            signals = [
                recv_ref[chunk, pl.ds(at + i + SUB * signal, N, stride=ROWS), :]
                for i in range(2)
                for signal in range(2)
            ]
            spectra = ahead(signals)
            mixed = []
            for i in range(2):
                product, grad = spectra[2 * i], spectra[2 * i + 1]
                filt = (spec_ref[chunk, at + i, 0], spec_ref[chunk, at + i, 1])
                mixed.append(times(filt, product))
                mixed.append(conj_times(filt, grad))
                mixed.append(conj_times(product, grad))
            results = inverse(
                mixed, last_ref[...], middle_ref[2], middle_ref[3], turn_ref[0], turn_ref[1]
            )
            for i in range(2):
                out_ref[chunk, pl.ds(at + i, N, stride=ROWS), :] = columns(results, 3 * i)
                out_ref[chunk, pl.ds(at + i + SUB, N, stride=ROWS), :] = columns(
                    results, 3 * i + 1
                )
                own_ref[chunk, pl.ds(at + i, N, stride=SUB), :] = columns(results, 3 * i + 2)

    def pair_copy(chunk):
        return pltpu.make_async_remote_copy(
            src_ref=own_ref.at[chunk, taps, :],
            dst_ref=other_ref.at[chunk],
            send_sem=pair_send.at[chunk],
            recv_sem=pair_recv.at[chunk],
            device_id=(1 - pair, me),
            device_id_type=MESH,
        )

    for chunk in range(CHUNKS):
        await_all(chunk, recv_ref, in_recv)
        convolve(chunk)
        send_all(chunk, out_ref, back_ref, out_send, out_recv)
        pair_copy(chunk).start()

    for chunk in range(CHUNKS):
        pair_copy(chunk).wait()
    grad_f_ref[...] = (own_ref[:, taps, :] + other_ref[...]) * scale

    await_all(0, back_ref, out_recv)
    results = (gated_ref, grad_q_ref, grad_k_ref, grad_v_ref)

    @pl.loop(0, size, unroll=4)
    def _(peer):
        gate(0, peer, (q_ref, c_ref, v_ref, k_ref), back_ref, results)

    for chunk in range(CHUNKS):
        await_all(chunk, send_ref, in_send)
        await_all(chunk, out_ref, out_send)
    await_all(1, back_ref, out_recv)


def store_kernel(
    pieces,
    back_ref, grad_f_ref, gated_ref, grad_q_ref, grad_k_ref, grad_v_ref,
    q_ref, k_ref, v_ref, c_ref,
    gated_hbm, grad_q_hbm, grad_k_hbm, grad_v_hbm, grad_f_hbm,
    late_gated, late_grad_q, late_grad_k, late_grad_v, sems,
):
    block = q_ref.shape[0] // pieces
    early = (gated_ref, grad_q_ref, grad_k_ref, grad_v_ref)
    late = (late_gated, late_grad_q, late_grad_k, late_grad_v)
    targets = (gated_hbm, grad_q_hbm, grad_k_hbm, grad_v_hbm)
    stores = []

    def store(source, target):
        copy = pltpu.make_async_copy(source, target, sems.at[len(stores)])
        copy.start()
        stores.append(copy)

    for source, target in zip(early, targets):
        store(source, target.at[:, 0])
    store(grad_f_ref, grad_f_hbm)
    for piece in range(pieces):
        @pl.loop(piece * block, (piece + 1) * block, unroll=4)
        def _(peer):
            gate(1, peer, (q_ref, c_ref, v_ref, k_ref), back_ref, late)

        part = pl.ds(piece * block, block)
        for source, target in zip(late, targets):
            store(source.at[part], target.at[part, 1])
    for copy in stores:
        copy.wait()


def on_device(query_input, key_input, value_input, filters, cotangent):
    size = lax.axis_size("context")
    channels = query_input.shape[1]
    rows, length = filters.shape
    scale = 1.0 / math.sqrt(lax.axis_size("dp") * length)
    token_shape = (size, CHUNKS, SUB, LANES)
    tokens = [
        array.reshape(token_shape) for array in (query_input, key_input, value_input, cotangent)
    ]
    taps = filters.reshape(CHUNKS, SUB, size, LANES).transpose(0, 2, 1, 3)
    taps = taps.reshape(CHUNKS, size * SUB, LANES)
    constants = [jnp.asarray(table) for table in tables()]

    hbm_spec = pl.BlockSpec(memory_space=pltpu.HBM)
    vmem_spec = pl.BlockSpec(memory_space=pltpu.VMEM)
    wide = (CHUNKS, size * ROWS, LANES)
    narrow = (CHUNKS, size * SUB, LANES)
    wide_strided = (CHUNKS, (size + 1) * ROWS, LANES)
    narrow_strided = (CHUNKS, (size + 1) * SUB, LANES)
    half = (size, SUB, LANES)
    per_chunk = pltpu.SemaphoreType.DMA((CHUNKS,))
    def pinned(array):
        return pltpu.with_memory_space_constraint(array, pltpu.HBM)

    held = pl.pallas_call(
        functools.partial(exchange_kernel, size, scale),
        out_shape=[
            pltpu.VMEM(shape, F32) for shape in [wide, narrow] + [half] * 4 + [token_shape] * 4
        ],
        in_specs=[hbm_spec] * 9,
        out_specs=[vmem_spec] * 10,
        scratch_shapes=[pltpu.VMEM(shape, F32) for shape in (narrow_strided, narrow, narrow_strided)]
        + [pltpu.VMEM(table.shape, table.dtype) for table in constants]
        + [
            pltpu.VMEM((2 * N, 3 * N), BF16),
            pltpu.VMEM((N, 6 * N), BF16),
            pltpu.VMEM((4, 2 * N, 2 * N), BF16),
            pltpu.VMEM(wide, F32),
            pltpu.VMEM(wide_strided, F32),
            pltpu.VMEM(wide_strided, F32),
            pltpu.VMEM((CHUNKS, SUB, 2, N, LANES), F32),
            pltpu.SemaphoreType.DMA((4 * CHUNKS + 5,)),
            pltpu.SemaphoreType.REGULAR((LINE // 2,)),
        ]
        + [per_chunk] * 6,
        compiler_params=pltpu.CompilerParams(
            collective_id=0, has_side_effects=True, vmem_limit_bytes=40 * 2**20
        ),
        name="exchange",
    )(*map(pinned, (*tokens, taps, *constants)))

    pieces = 2
    results = pl.pallas_call(
        functools.partial(store_kernel, pieces),
        out_shape=[jax.ShapeDtypeStruct(token_shape, F32)] * 4
        + [jax.ShapeDtypeStruct(narrow, F32)],
        in_specs=[vmem_spec] * 10,
        out_specs=[hbm_spec] * 5,
        scratch_shapes=[pltpu.VMEM(half, F32) for _ in range(4)]
        + [pltpu.SemaphoreType.DMA((5 + 4 * pieces,))],
        compiler_params=pltpu.CompilerParams(vmem_limit_bytes=20 * 2**20),
        name="store",
    )(*held)
    per_token = [array.reshape(1, channels, LANES) for array in results[:4]]
    grad_filter = results[4].reshape(CHUNKS, size, SUB, LANES).transpose(0, 2, 1, 3)
    return (*per_token, grad_filter.reshape(rows, length))


def solution(mesh):
    token = P("dp", None, "context")
    taps = P("context", None)
    return jax.shard_map(
        on_device,
        mesh=mesh,
        in_specs=(token, token, token, taps, token),
        out_specs=(token, token, token, token, taps),
        check_vma=False,
    )
```

```python
import functools
import math

import jax
import jax.numpy as jnp
import numpy as np
from jax import lax
from jax.experimental import pallas as pl
from jax.experimental.pallas import tpu as pltpu
from jax.sharding import PartitionSpec as P

MESH = pl.DeviceIdType.MESH
F32 = jnp.float32
BF16 = jnp.bfloat16
N = 128
SUB = 8
CHUNKS = 2
ROWS = 2 * SUB
LANES = 128
STRIDE, LINE = 4, 8


def tables():
    steps = np.arange(N, dtype=np.float64)
    total = N * N
    outer = 2.0 * math.pi / N * (steps[:, None] + 0.25) * steps[None, :]
    twist = 2.0 * math.pi / total * (steps[:, None] + 0.25) * steps[None, :]
    inner = 2.0 * math.pi / N * ((steps[:, None] * steps[None, :]) % N)
    first = np.concatenate([np.cos(outer), -np.sin(outer)], axis=0)
    last = np.concatenate([np.cos(outer.T), -np.sin(outer.T)], axis=1) / total
    cos, sin = np.cos(inner), np.sin(inner)
    middle = np.stack([np.block([[cos, -sin], [sin, cos]]), np.block([[cos, sin], [-sin, cos]])])
    turn = np.stack([np.cos(twist), np.sin(twist)])
    return [table.astype(np.float32) for table in (first, last, middle, turn)]


def split(value):
    high = value.astype(BF16)
    rest = value - high.astype(F32)
    mid = rest.astype(BF16)
    low = (rest - mid.astype(F32)).astype(BF16)
    return high, mid, low


def stacked_rows(value):
    high, mid, low = split(value)
    return jnp.concatenate([high, high, high, mid, mid, low], axis=0)


def dot(left, right):
    return jnp.dot(left, right, preferred_element_type=F32)


def columns(value, index):
    return value[:, index * LANES : (index + 1) * LANES]


def by_inner(pairs, table):
    stacked = jnp.concatenate([jnp.concatenate(pair, axis=1) for pair in pairs], axis=0)
    high, mid, low = split(stacked)
    result = dot(high, table[0]) + dot(high, table[1]) + dot(high, table[2])
    result += dot(mid, table[0]) + dot(mid, table[1]) + dot(low, table[0])
    return [
        (result[i * N : (i + 1) * N, :N], result[i * N : (i + 1) * N, N:])
        for i in range(len(pairs))
    ]


def forward(signals, first, table, cos, sin):
    mixed = dot(first, stacked_rows(jnp.concatenate(signals, axis=1)))
    pairs = []
    for i in range(len(signals)):
        re, im = columns(mixed[:N], i), columns(mixed[N:], i)
        pairs.append((re * cos + im * sin, im * cos - re * sin))
    return by_inner(pairs, table)


def inverse(spectra, last, table, cos, sin):
    turned_re, turned_im = [], []
    for re, im in by_inner(spectra, table):
        turned_re.append(re * cos - im * sin)
        turned_im.append(re * sin + im * cos)
    stacked = jnp.concatenate(
        [jnp.concatenate(turned_re, axis=1), jnp.concatenate(turned_im, axis=1)], axis=0
    )
    return dot(last, stacked_rows(stacked))


def times(a, b):
    return (a[0] * b[0] - a[1] * b[1], a[0] * b[1] + a[1] * b[0])


def conj_times(a, b):
    return (a[0] * b[0] + a[1] * b[1], a[0] * b[1] - a[1] * b[0])


def gate(chunk, peer, factors, back_ref, results):
    base = pl.multiple_of(peer * ROWS, ROWS)
    conv = back_ref[chunk, pl.ds(base, SUB), :]
    back = back_ref[chunk, pl.ds(base + SUB, SUB), :]
    for factor, signal, result in zip(factors, (conv, conv, back, back), results):
        result[peer] = factor[peer, chunk] * signal


def exchange_kernel(
    size, scale,
    q_hbm, k_hbm, v_hbm, c_hbm, filt_hbm, first_hbm, last_hbm, middle_hbm, turn_hbm,
    back_ref, grad_f_ref, gated_ref, grad_q_ref, grad_k_ref, grad_v_ref,
    q_ref, k_ref, v_ref, c_ref,
    own_ref, other_ref, filt_ref, first_f32, last_f32, middle_f32, turn_ref,
    first_ref, last_ref, middle_ref, send_ref, recv_ref, out_ref, spec_ref,
    load_sems, wave_sem, in_send, in_recv, out_send, out_recv, pair_send, pair_recv,
):
    me = lax.axis_index("context")
    pair = lax.axis_index("dp")
    taps = pl.ds(0, size * SUB)

    planes = size // LINE
    place = lax.rem(me // STRIDE, LINE)
    spot = me // (STRIDE * LINE) * STRIDE + lax.rem(me, STRIDE)

    def peer_at(line, plane):
        z = place + line
        z = jnp.where(z >= LINE, z - LINE, z)
        at = spot + plane
        at = jnp.where(at >= planes, at - planes, at)
        return (at // STRIDE * LINE + z) * STRIDE + lax.rem(at, STRIDE)

    def loader(i, source, target):
        return pltpu.make_async_copy(source, target, load_sems.at[i])

    loads = [
        loader(i, source, target)
        for i, (source, target) in enumerate(
            [
                (source.at[:, chunk], target.at[:, chunk])
                for chunk in range(CHUNKS)
                for source, target in (
                    (k_hbm, k_ref), (v_hbm, v_ref), (c_hbm, c_ref), (q_hbm, q_ref)
                )
            ]
            + [
                (filt_hbm, filt_ref.at[:, taps, :]), (first_hbm, first_f32), (last_hbm, last_f32),
                (middle_hbm, middle_f32), (turn_hbm, turn_ref),
            ]
        )
    ]
    for load in loads[:4]:
        load.start()

    barrier = pltpu.get_barrier_semaphore()

    def greet(semaphore, peer):
        pl.semaphore_signal(semaphore, inc=1, device_id=(pair, peer), device_id_type=MESH)

    for plane in range(1, planes):
        greet(barrier, peer_at(0, plane))
    for line in (1, LINE - 1):
        greet(barrier, peer_at(line, 0))
    pl.semaphore_signal(barrier, inc=1, device_id=(1 - pair, me), device_id_type=MESH)
    for load in loads[4:]:
        load.start()

    def tell(stage):
        for line in (1, LINE - 1):
            greet(wave_sem.at[stage], peer_at(line, 0))

    pl.semaphore_wait(barrier, planes + 2)
    tell(0)
    for load in loads[:4]:
        load.wait()

    def rows_of(peer):
        return pl.ds(pl.multiple_of(peer * ROWS, ROWS), ROWS)

    def products(chunk):
        @pl.loop(0, size, unroll=8)
        def _(peer):
            base = pl.multiple_of(peer * ROWS, ROWS)
            send_ref[chunk, pl.ds(base, SUB), :] = k_ref[peer, chunk] * v_ref[peer, chunk]
            send_ref[chunk, pl.ds(base + SUB, SUB), :] = c_ref[peer, chunk] * q_ref[peer, chunk]

    def sender(chunk, source, target, send_sem, recv_sem):
        def send(line, plane):
            peer = peer_at(line, plane)
            pltpu.make_async_remote_copy(
                src_ref=source.at[chunk, rows_of(peer), :],
                dst_ref=target.at[chunk, rows_of(me), :],
                send_sem=send_sem.at[chunk],
                recv_sem=recv_sem.at[chunk],
                device_id=(pair, peer),
                device_id_type=MESH,
            ).start()

        return send

    def keep(chunk, source, target):
        target[chunk, rows_of(me), :] = source[chunk, rows_of(me), :]

    def send_plane(send, line):
        @pl.loop(0, planes)
        def _(plane):
            send(line, plane)

    def send_own_plane(send):
        @pl.loop(1, planes)
        def _(plane):
            send(0, plane)

    def send_all(chunk, source, target, send_sem, recv_sem):
        keep(chunk, source, target)
        send = sender(chunk, source, target, send_sem, recv_sem)
        for line in (4, 1, 7, 2, 6, 3, 5):
            send(line, 0)

        @pl.loop(1, planes)
        def _(plane):
            for line in (4, 1, 7, 2, 0, 6, 3, 5):
                send(line, plane)

    def await_all(chunk, ref, sem):
        part = ref.at[chunk, pl.ds(0, (size - 1) * ROWS), :]
        pltpu.make_async_copy(part, part, sem.at[chunk]).wait()

    products(0)
    keep(0, send_ref, recv_ref)
    send = sender(0, send_ref, recv_ref, in_send, in_recv)
    for stage in range(1, LINE // 2):
        pl.semaphore_wait(wave_sem.at[stage - 1], 2)
        tell(stage)
        send_plane(send, stage)
        send_plane(send, LINE - stage)
    pl.semaphore_wait(wave_sem.at[LINE // 2 - 1], 2)
    send_plane(send, LINE // 2)
    send_own_plane(send)
    for load in loads[4:8]:
        load.wait()
    products(1)
    send_all(1, send_ref, recv_ref, in_send, in_recv)

    for load in loads[8:]:
        load.wait()

    def stacked_columns(table):
        high, mid, low = split(table)
        return jnp.concatenate([high, mid, low, high, mid, high], axis=1)

    first_ref[...] = stacked_columns(first_f32[...])
    last_ref[...] = stacked_columns(last_f32[...])
    for way in range(2):
        for i, piece in enumerate(split(middle_f32[way])):
            middle_ref[way, i] = piece

    def ahead(signals):
        return forward(
            signals, first_ref[...], middle_ref.at[0], turn_ref[0], turn_ref[1]
        )

    for chunk in range(CHUNKS):
        @pl.loop(0, SUB // 4)
        def _(step):
            at = step * 4
            signals = [filt_ref[chunk, pl.ds(at + i, N, stride=SUB), :] for i in range(4)]
            for i, (re, im) in enumerate(ahead(signals)):
                spec_ref[chunk, at + i, 0] = re
                spec_ref[chunk, at + i, 1] = im

    def convolve(chunk):
        @pl.loop(0, SUB // 2)
        def _(step):
            at = step * 2
            signals = [
                recv_ref[chunk, pl.ds(at + i + SUB * signal, N, stride=ROWS), :]
                for i in range(2)
                for signal in range(2)
            ]
            spectra = ahead(signals)
            mixed = []
            for i in range(2):
                product, grad = spectra[2 * i], spectra[2 * i + 1]
                filt = (spec_ref[chunk, at + i, 0], spec_ref[chunk, at + i, 1])
                mixed.append(times(filt, product))
                mixed.append(conj_times(filt, grad))
                mixed.append(conj_times(product, grad))
            results = inverse(
                mixed, last_ref[...], middle_ref.at[1], turn_ref[0], turn_ref[1]
            )
            for i in range(2):
                out_ref[chunk, pl.ds(at + i, N, stride=ROWS), :] = columns(results, 3 * i)
                out_ref[chunk, pl.ds(at + i + SUB, N, stride=ROWS), :] = columns(
                    results, 3 * i + 1
                )
                own_ref[chunk, pl.ds(at + i, N, stride=SUB), :] = columns(results, 3 * i + 2)

    def pair_copy(chunk):
        return pltpu.make_async_remote_copy(
            src_ref=own_ref.at[chunk, taps, :],
            dst_ref=other_ref.at[chunk],
            send_sem=pair_send.at[chunk],
            recv_sem=pair_recv.at[chunk],
            device_id=(1 - pair, me),
            device_id_type=MESH,
        )

    for chunk in range(CHUNKS):
        await_all(chunk, recv_ref, in_recv)
        convolve(chunk)
        send_all(chunk, out_ref, back_ref, out_send, out_recv)
        pair_copy(chunk).start()

    for chunk in range(CHUNKS):
        pair_copy(chunk).wait()
    grad_f_ref[...] = (own_ref[:, taps, :] + other_ref[...]) * scale

    await_all(0, back_ref, out_recv)
    results = (gated_ref, grad_q_ref, grad_k_ref, grad_v_ref)

    @pl.loop(0, size, unroll=4)
    def _(peer):
        gate(0, peer, (q_ref, c_ref, v_ref, k_ref), back_ref, results)

    for chunk in range(CHUNKS):
        await_all(chunk, send_ref, in_send)
        await_all(chunk, out_ref, out_send)
    await_all(1, back_ref, out_recv)


def store_kernel(
    pieces,
    back_ref, grad_f_ref, gated_ref, grad_q_ref, grad_k_ref, grad_v_ref,
    q_ref, k_ref, v_ref, c_ref,
    gated_hbm, grad_q_hbm, grad_k_hbm, grad_v_hbm, grad_f_hbm,
    late_gated, late_grad_q, late_grad_k, late_grad_v, sems,
):
    block = q_ref.shape[0] // pieces
    early = (gated_ref, grad_q_ref, grad_k_ref, grad_v_ref)
    late = (late_gated, late_grad_q, late_grad_k, late_grad_v)
    targets = (gated_hbm, grad_q_hbm, grad_k_hbm, grad_v_hbm)
    stores = []

    def store(source, target):
        copy = pltpu.make_async_copy(source, target, sems.at[len(stores)])
        copy.start()
        stores.append(copy)

    for source, target in zip(early, targets):
        store(source, target.at[:, 0])
    store(grad_f_ref, grad_f_hbm)
    for piece in range(pieces):
        @pl.loop(piece * block, (piece + 1) * block, unroll=4)
        def _(peer):
            gate(1, peer, (q_ref, c_ref, v_ref, k_ref), back_ref, late)

        part = pl.ds(piece * block, block)
        for source, target in zip(late, targets):
            store(source.at[part], target.at[part, 1])
    for copy in stores:
        copy.wait()


def on_device(query_input, key_input, value_input, filters, cotangent):
    size = lax.axis_size("context")
    channels = query_input.shape[1]
    rows, length = filters.shape
    scale = 1.0 / math.sqrt(lax.axis_size("dp") * length)
    token_shape = (size, CHUNKS, SUB, LANES)
    tokens = [
        array.reshape(token_shape) for array in (query_input, key_input, value_input, cotangent)
    ]
    taps = filters.reshape(CHUNKS, SUB, size, LANES).transpose(0, 2, 1, 3)
    taps = taps.reshape(CHUNKS, size * SUB, LANES)
    constants = [jnp.asarray(table) for table in tables()]

    hbm_spec = pl.BlockSpec(memory_space=pltpu.HBM)
    vmem_spec = pl.BlockSpec(memory_space=pltpu.VMEM)
    wide = (CHUNKS, size * ROWS, LANES)
    narrow = (CHUNKS, size * SUB, LANES)
    wide_strided = (CHUNKS, (size + 1) * ROWS, LANES)
    narrow_strided = (CHUNKS, (size + 1) * SUB, LANES)
    half = (size, SUB, LANES)
    per_chunk = pltpu.SemaphoreType.DMA((CHUNKS,))
    def pinned(array):
        return pltpu.with_memory_space_constraint(array, pltpu.HBM)

    held = pl.pallas_call(
        functools.partial(exchange_kernel, size, scale),
        out_shape=[
            pltpu.VMEM(shape, F32) for shape in [wide, narrow] + [half] * 4 + [token_shape] * 4
        ],
        in_specs=[hbm_spec] * 9,
        out_specs=[vmem_spec] * 10,
        scratch_shapes=[pltpu.VMEM(shape, F32) for shape in (narrow_strided, narrow, narrow_strided)]
        + [pltpu.VMEM(table.shape, table.dtype) for table in constants]
        + [
            pltpu.VMEM((2 * N, 6 * N), BF16),
            pltpu.VMEM((N, 12 * N), BF16),
            pltpu.VMEM((2, 3, 2 * N, 2 * N), BF16),
            pltpu.VMEM(wide, F32),
            pltpu.VMEM(wide_strided, F32),
            pltpu.VMEM(wide_strided, F32),
            pltpu.VMEM((CHUNKS, SUB, 2, N, LANES), F32),
            pltpu.SemaphoreType.DMA((4 * CHUNKS + 5,)),
            pltpu.SemaphoreType.REGULAR((LINE // 2,)),
        ]
        + [per_chunk] * 6,
        compiler_params=pltpu.CompilerParams(
            collective_id=0, has_side_effects=True, vmem_limit_bytes=40 * 2**20
        ),
        name="exchange",
    )(*map(pinned, (*tokens, taps, *constants)))

    pieces = 2
    results = pl.pallas_call(
        functools.partial(store_kernel, pieces),
        out_shape=[jax.ShapeDtypeStruct(token_shape, F32)] * 4
        + [jax.ShapeDtypeStruct(narrow, F32)],
        in_specs=[vmem_spec] * 10,
        out_specs=[hbm_spec] * 5,
        scratch_shapes=[pltpu.VMEM(half, F32) for _ in range(4)]
        + [pltpu.SemaphoreType.DMA((5 + 4 * pieces,))],
        compiler_params=pltpu.CompilerParams(vmem_limit_bytes=20 * 2**20),
        name="store",
    )(*held)
    per_token = [array.reshape(1, channels, LANES) for array in results[:4]]
    grad_filter = results[4].reshape(CHUNKS, size, SUB, LANES).transpose(0, 2, 1, 3)
    return (*per_token, grad_filter.reshape(rows, length))


def solution(mesh):
    token = P("dp", None, "context")
    taps = P("context", None)
    return jax.shard_map(
        on_device,
        mesh=mesh,
        in_specs=(token, token, token, taps, token),
        out_specs=(token, token, token, token, taps),
        check_vma=False,
    )
```

```python
import functools
import math

import jax
import jax.numpy as jnp
import numpy as np
from jax import lax
from jax.experimental import pallas as pl
from jax.experimental.pallas import tpu as pltpu
from jax.sharding import PartitionSpec as P

MESH = pl.DeviceIdType.MESH
F32 = jnp.float32
BF16 = jnp.bfloat16
N = 128
SUB = 8
CHUNKS = 2
ROWS = 2 * SUB
LANES = 128
STRIDE, LINE = 4, 8


def tables():
    steps = np.arange(N, dtype=np.float64)
    total = N * N
    outer = 2.0 * math.pi / N * (steps[:, None] + 0.25) * steps[None, :]
    twist = 2.0 * math.pi / total * (steps[:, None] + 0.25) * steps[None, :]
    inner = 2.0 * math.pi / N * ((steps[:, None] * steps[None, :]) % N)
    first = np.concatenate([np.cos(outer), -np.sin(outer)], axis=0)
    last = np.concatenate([np.cos(outer.T), -np.sin(outer.T)], axis=1) / total
    cos, sin = np.cos(inner), np.sin(inner)
    middle = np.stack([np.block([[cos, -sin], [sin, cos]]), np.block([[cos, sin], [-sin, cos]])])
    turn = np.stack([np.cos(twist), np.sin(twist)])
    return [table.astype(np.float32) for table in (first, last, middle, turn)]


def split(value):
    high = value.astype(BF16)
    rest = value - high.astype(F32)
    mid = rest.astype(BF16)
    low = (rest - mid.astype(F32)).astype(BF16)
    return high, mid, low


def stacked_rows(value):
    high, mid, low = split(value)
    return jnp.concatenate([high, high, high, mid, mid, low], axis=0)


def dot(left, right):
    return jnp.dot(left, right, preferred_element_type=F32)


def columns(value, index):
    return value[:, index * LANES : (index + 1) * LANES]


def by_inner(pairs, table):
    stacked = jnp.concatenate([jnp.concatenate(pair, axis=1) for pair in pairs], axis=0)
    high, mid, low = split(stacked)
    result = dot(high, table[0]) + dot(high, table[1]) + dot(high, table[2])
    result += dot(mid, table[0]) + dot(mid, table[1]) + dot(low, table[0])
    return [
        (result[i * N : (i + 1) * N, :N], result[i * N : (i + 1) * N, N:])
        for i in range(len(pairs))
    ]


def forward(signals, first, table, cos, sin):
    mixed = dot(first, stacked_rows(jnp.concatenate(signals, axis=1)))
    pairs = []
    for i in range(len(signals)):
        re, im = columns(mixed[:N], i), columns(mixed[N:], i)
        pairs.append((re * cos + im * sin, im * cos - re * sin))
    return by_inner(pairs, table)


def inverse(spectra, last, table, cos, sin):
    turned_re, turned_im = [], []
    for re, im in by_inner(spectra, table):
        turned_re.append(re * cos - im * sin)
        turned_im.append(re * sin + im * cos)
    stacked = jnp.concatenate(
        [jnp.concatenate(turned_re, axis=1), jnp.concatenate(turned_im, axis=1)], axis=0
    )
    return dot(last, stacked_rows(stacked))


def times(a, b):
    return (a[0] * b[0] - a[1] * b[1], a[0] * b[1] + a[1] * b[0])


def conj_times(a, b):
    return (a[0] * b[0] + a[1] * b[1], a[0] * b[1] - a[1] * b[0])


def gate(chunk, peer, factors, back_ref, results):
    base = pl.multiple_of(peer * ROWS, ROWS)
    conv = back_ref[chunk, pl.ds(base, SUB), :]
    back = back_ref[chunk, pl.ds(base + SUB, SUB), :]
    for factor, signal, result in zip(factors, (conv, conv, back, back), results):
        result[peer] = factor[peer, chunk] * signal


def exchange_kernel(
    size, scale,
    q_hbm, k_hbm, v_hbm, c_hbm, filt_hbm, first_hbm, last_hbm, middle_hbm, turn_hbm,
    back_ref, grad_f_ref, gated_ref, grad_q_ref, grad_k_ref, grad_v_ref,
    q_ref, k_ref, v_ref, c_ref,
    own_ref, other_ref, filt_ref, first_f32, last_f32, middle_f32, turn_ref,
    first_ref, last_ref, middle_ref, send_ref, recv_ref, out_ref, spec_ref,
    load_sems, wave_sem, in_send, in_recv, out_send, out_recv, pair_send, pair_recv,
):
    me = lax.axis_index("context")
    pair = lax.axis_index("dp")
    taps = pl.ds(0, size * SUB)

    planes = size // LINE
    place = lax.rem(me // STRIDE, LINE)
    spot = me // (STRIDE * LINE) * STRIDE + lax.rem(me, STRIDE)

    def peer_at(line, plane):
        z = place + line
        z = jnp.where(z >= LINE, z - LINE, z)
        at = spot + plane
        at = jnp.where(at >= planes, at - planes, at)
        return (at // STRIDE * LINE + z) * STRIDE + lax.rem(at, STRIDE)

    def peer_on(z, plane):
        at = spot + plane
        at = jnp.where(at >= planes, at - planes, at)
        return (at // STRIDE * LINE + z) * STRIDE + lax.rem(at, STRIDE)

    def loader(i, source, target):
        return pltpu.make_async_copy(source, target, load_sems.at[i])

    loads = [
        loader(i, source, target)
        for i, (source, target) in enumerate(
            [
                (source.at[:, chunk], target.at[:, chunk])
                for chunk in range(CHUNKS)
                for source, target in (
                    (k_hbm, k_ref), (v_hbm, v_ref), (c_hbm, c_ref), (q_hbm, q_ref)
                )
            ]
            + [
                (filt_hbm, filt_ref.at[:, taps, :]), (first_hbm, first_f32), (last_hbm, last_f32),
                (middle_hbm, middle_f32), (turn_hbm, turn_ref),
            ]
        )
    ]
    for load in loads[:4]:
        load.start()

    barrier = pltpu.get_barrier_semaphore()

    def greet(semaphore, peer):
        pl.semaphore_signal(semaphore, inc=1, device_id=(pair, peer), device_id_type=MESH)

    for plane in range(1, planes):
        greet(barrier, peer_at(0, plane))
    for line in (1, LINE - 1):
        greet(barrier, peer_at(line, 0))
    pl.semaphore_signal(barrier, inc=1, device_id=(1 - pair, me), device_id_type=MESH)
    for load in loads[4:]:
        load.start()

    def tell(stage):
        for line in (1, LINE - 1):
            greet(wave_sem.at[stage], peer_at(line, 0))

    pl.semaphore_wait(barrier, planes + 2)
    tell(0)
    for load in loads[:4]:
        load.wait()

    def rows_of(peer):
        return pl.ds(pl.multiple_of(peer * ROWS, ROWS), ROWS)

    def products(chunk):
        @pl.loop(0, size, unroll=8)
        def _(peer):
            base = pl.multiple_of(peer * ROWS, ROWS)
            send_ref[chunk, pl.ds(base, SUB), :] = k_ref[peer, chunk] * v_ref[peer, chunk]
            send_ref[chunk, pl.ds(base + SUB, SUB), :] = c_ref[peer, chunk] * q_ref[peer, chunk]

    def sender(chunk, source, target, send_sem, recv_sem, find=peer_at):
        def send(line, plane):
            peer = find(line, plane)
            pltpu.make_async_remote_copy(
                src_ref=source.at[chunk, rows_of(peer), :],
                dst_ref=target.at[chunk, rows_of(me), :],
                send_sem=send_sem.at[chunk],
                recv_sem=recv_sem.at[chunk],
                device_id=(pair, peer),
                device_id_type=MESH,
            ).start()

        return send

    def keep(chunk, source, target):
        target[chunk, rows_of(me), :] = source[chunk, rows_of(me), :]

    def send_plane(send, line):
        @pl.loop(0, planes)
        def _(plane):
            send(line, plane)

    def send_own_plane(send):
        @pl.loop(1, planes)
        def _(plane):
            send(0, plane)

    def send_all(chunk, source, target, send_sem, recv_sem, last=False):
        keep(chunk, source, target)
        send = sender(chunk, source, target, send_sem, recv_sem)
        for line in (4, 1, 7, 2, 6, 3, 5):
            send(line, 0)

        if last:
            send = sender(chunk, source, target, send_sem, recv_sem, peer_on)
            for group in ((0, 4, 1, 6, 2), (7, 3, 5)):
                @pl.loop(1, planes)
                def _(plane):
                    for z in group:
                        send(z, plane)
        else:
            @pl.loop(1, planes)
            def _(plane):
                for line in (4, 1, 7, 2, 0, 6, 3, 5):
                    send(line, plane)

    def await_all(chunk, ref, sem):
        part = ref.at[chunk, pl.ds(0, (size - 1) * ROWS), :]
        pltpu.make_async_copy(part, part, sem.at[chunk]).wait()

    products(0)
    keep(0, send_ref, recv_ref)
    send = sender(0, send_ref, recv_ref, in_send, in_recv)
    for stage in range(1, LINE // 2):
        pl.semaphore_wait(wave_sem.at[stage - 1], 2)
        tell(stage)
        send_plane(send, stage)
        send_plane(send, LINE - stage)
    pl.semaphore_wait(wave_sem.at[LINE // 2 - 1], 2)
    send_plane(send, LINE // 2)
    send_own_plane(send)
    for load in loads[4:8]:
        load.wait()
    products(1)
    send_all(1, send_ref, recv_ref, in_send, in_recv)

    for load in loads[8:]:
        load.wait()

    def stacked_columns(table):
        high, mid, low = split(table)
        return jnp.concatenate([high, mid, low, high, mid, high], axis=1)

    first_ref[...] = stacked_columns(first_f32[...])
    last_ref[...] = stacked_columns(last_f32[...])
    for way in range(2):
        for i, piece in enumerate(split(middle_f32[way])):
            middle_ref[way, i] = piece

    def ahead(signals):
        return forward(
            signals, first_ref[...], middle_ref.at[0], turn_ref[0], turn_ref[1]
        )

    for chunk in range(CHUNKS):
        @pl.loop(0, SUB // 4)
        def _(step):
            at = step * 4
            signals = [filt_ref[chunk, pl.ds(at + i, N, stride=SUB), :] for i in range(4)]
            for i, (re, im) in enumerate(ahead(signals)):
                spec_ref[chunk, at + i, 0] = re
                spec_ref[chunk, at + i, 1] = im

    def convolve(chunk):
        @pl.loop(0, SUB // 2)
        def _(step):
            at = step * 2
            signals = [
                recv_ref[chunk, pl.ds(at + i + SUB * signal, N, stride=ROWS), :]
                for i in range(2)
                for signal in range(2)
            ]
            spectra = ahead(signals)
            mixed = []
            for i in range(2):
                product, grad = spectra[2 * i], spectra[2 * i + 1]
                filt = (spec_ref[chunk, at + i, 0], spec_ref[chunk, at + i, 1])
                mixed.append(times(filt, product))
                mixed.append(conj_times(filt, grad))
                mixed.append(conj_times(product, grad))
            results = inverse(
                mixed, last_ref[...], middle_ref.at[1], turn_ref[0], turn_ref[1]
            )
            for i in range(2):
                out_ref[chunk, pl.ds(at + i, N, stride=ROWS), :] = columns(results, 3 * i)
                out_ref[chunk, pl.ds(at + i + SUB, N, stride=ROWS), :] = columns(
                    results, 3 * i + 1
                )
                own_ref[chunk, pl.ds(at + i, N, stride=SUB), :] = columns(results, 3 * i + 2)

    def pair_copy(chunk):
        return pltpu.make_async_remote_copy(
            src_ref=own_ref.at[chunk, taps, :],
            dst_ref=other_ref.at[chunk],
            send_sem=pair_send.at[chunk],
            recv_sem=pair_recv.at[chunk],
            device_id=(1 - pair, me),
            device_id_type=MESH,
        )

    for chunk in range(CHUNKS):
        await_all(chunk, recv_ref, in_recv)
        convolve(chunk)
        send_all(chunk, out_ref, back_ref, out_send, out_recv, chunk == CHUNKS - 1)
        pair_copy(chunk).start()

    for chunk in range(CHUNKS):
        pair_copy(chunk).wait()
    grad_f_ref[...] = (own_ref[:, taps, :] + other_ref[...]) * scale

    await_all(0, back_ref, out_recv)
    results = (gated_ref, grad_q_ref, grad_k_ref, grad_v_ref)

    @pl.loop(0, size, unroll=4)
    def _(peer):
        gate(0, peer, (q_ref, c_ref, v_ref, k_ref), back_ref, results)

    for chunk in range(CHUNKS):
        await_all(chunk, send_ref, in_send)
        await_all(chunk, out_ref, out_send)
    await_all(1, back_ref, out_recv)


def store_kernel(
    pieces,
    back_ref, grad_f_ref, gated_ref, grad_q_ref, grad_k_ref, grad_v_ref,
    q_ref, k_ref, v_ref, c_ref,
    gated_hbm, grad_q_hbm, grad_k_hbm, grad_v_hbm, grad_f_hbm,
    late_gated, late_grad_q, late_grad_k, late_grad_v, sems,
):
    block = q_ref.shape[0] // pieces
    early = (gated_ref, grad_q_ref, grad_k_ref, grad_v_ref)
    late = (late_gated, late_grad_q, late_grad_k, late_grad_v)
    targets = (gated_hbm, grad_q_hbm, grad_k_hbm, grad_v_hbm)
    stores = []

    def store(source, target):
        copy = pltpu.make_async_copy(source, target, sems.at[len(stores)])
        copy.start()
        stores.append(copy)

    for source, target in zip(early, targets):
        store(source, target.at[:, 0])
    store(grad_f_ref, grad_f_hbm)
    for piece in range(pieces):
        @pl.loop(piece * block, (piece + 1) * block, unroll=4)
        def _(peer):
            gate(1, peer, (q_ref, c_ref, v_ref, k_ref), back_ref, late)

        part = pl.ds(piece * block, block)
        for source, target in zip(late, targets):
            store(source.at[part], target.at[part, 1])
    for copy in stores:
        copy.wait()


def on_device(query_input, key_input, value_input, filters, cotangent):
    size = lax.axis_size("context")
    channels = query_input.shape[1]
    rows, length = filters.shape
    scale = 1.0 / math.sqrt(lax.axis_size("dp") * length)
    token_shape = (size, CHUNKS, SUB, LANES)
    tokens = [
        array.reshape(token_shape) for array in (query_input, key_input, value_input, cotangent)
    ]
    taps = filters.reshape(CHUNKS, SUB, size, LANES).transpose(0, 2, 1, 3)
    taps = taps.reshape(CHUNKS, size * SUB, LANES)
    constants = [jnp.asarray(table) for table in tables()]

    hbm_spec = pl.BlockSpec(memory_space=pltpu.HBM)
    vmem_spec = pl.BlockSpec(memory_space=pltpu.VMEM)
    wide = (CHUNKS, size * ROWS, LANES)
    narrow = (CHUNKS, size * SUB, LANES)
    wide_strided = (CHUNKS, (size + 1) * ROWS, LANES)
    narrow_strided = (CHUNKS, (size + 1) * SUB, LANES)
    half = (size, SUB, LANES)
    per_chunk = pltpu.SemaphoreType.DMA((CHUNKS,))
    def pinned(array):
        return pltpu.with_memory_space_constraint(array, pltpu.HBM)

    held = pl.pallas_call(
        functools.partial(exchange_kernel, size, scale),
        out_shape=[
            pltpu.VMEM(shape, F32) for shape in [wide, narrow] + [half] * 4 + [token_shape] * 4
        ],
        in_specs=[hbm_spec] * 9,
        out_specs=[vmem_spec] * 10,
        scratch_shapes=[pltpu.VMEM(shape, F32) for shape in (narrow_strided, narrow, narrow_strided)]
        + [pltpu.VMEM(table.shape, table.dtype) for table in constants]
        + [
            pltpu.VMEM((2 * N, 6 * N), BF16),
            pltpu.VMEM((N, 12 * N), BF16),
            pltpu.VMEM((2, 3, 2 * N, 2 * N), BF16),
            pltpu.VMEM(wide, F32),
            pltpu.VMEM(wide_strided, F32),
            pltpu.VMEM(wide_strided, F32),
            pltpu.VMEM((CHUNKS, SUB, 2, N, LANES), F32),
            pltpu.SemaphoreType.DMA((4 * CHUNKS + 5,)),
            pltpu.SemaphoreType.REGULAR((LINE // 2,)),
        ]
        + [per_chunk] * 6,
        compiler_params=pltpu.CompilerParams(
            collective_id=0, has_side_effects=True, vmem_limit_bytes=40 * 2**20
        ),
        name="exchange",
    )(*map(pinned, (*tokens, taps, *constants)))

    pieces = 2
    results = pl.pallas_call(
        functools.partial(store_kernel, pieces),
        out_shape=[jax.ShapeDtypeStruct(token_shape, F32)] * 4
        + [jax.ShapeDtypeStruct(narrow, F32)],
        in_specs=[vmem_spec] * 10,
        out_specs=[hbm_spec] * 5,
        scratch_shapes=[pltpu.VMEM(half, F32) for _ in range(4)]
        + [pltpu.SemaphoreType.DMA((5 + 4 * pieces,))],
        compiler_params=pltpu.CompilerParams(vmem_limit_bytes=20 * 2**20),
        name="store",
    )(*held)
    per_token = [array.reshape(1, channels, LANES) for array in results[:4]]
    grad_filter = results[4].reshape(CHUNKS, size, SUB, LANES).transpose(0, 2, 1, 3)
    return (*per_token, grad_filter.reshape(rows, length))


def solution(mesh):
    token = P("dp", None, "context")
    taps = P("context", None)
    return jax.shard_map(
        on_device,
        mesh=mesh,
        in_specs=(token, token, token, taps, token),
        out_specs=(token, token, token, token, taps),
        check_vma=False,
    )
```
